32 devices in a mesh: visit: 4 (over y, x), patch: 8 (over z, core).
Axes of the slice: x: 2, y: 2, z: 4, core: 2. Of those that a mesh axis runs over, the one named last changes fastest.
Arguments:
- pixels: bfloat16 [2048, 128, 128], P(('visit', 'patch')), may hold values from -6 to 6
- mask_bits: int32 [2048, 128, 128], P(('visit', 'patch')), may hold values from 0 to 15, as said below
- inv_var: float32 [2048], P(('visit', 'patch')), may hold values from 0.05 to 1
- owner: int32 [2048], P(('visit', 'patch')), may hold values from 0 to 7, as said below
- cell: int32 [2048], P(('visit', 'patch')), may hold values from 0 to 63
- coef_index: int32 [2048], P(('visit', 'patch')), may hold values from 0 to 63
- coef_table: float32 [64, 9], replicated, may hold values from -4 to 4
Outputs:
- coadd: float32 [512, 128, 128], P('patch', 'visit')
- difference: bfloat16 [2048, 128, 128], P(('visit', 'patch'))
The draws below stay inside these ranges and needn't reach their ends.
Inputs may be any that keep to these rules, and one draw needn't show every extreme that they name: `owner`: within each device's 64 blocks (aligned runs of 64 in order) no patch is named more than 32 times; one patch, the same for all devices, is named exactly 32 times in every such run. `mask_bits`: each value is a sum of the bit flags 1, 2, 4 and 8.
All inputs are finite; a program needn't handle non-finite values.
Results may differ from the reference program's by a relative error of at most 0.0071.
Values may be sent and summed in bfloat16 or wider, within the bound.
A program may use at most 128 MiB of HBM per device.

```python
import math
import jax
import jax.numpy as jnp
from jax import lax

BP = 128
BLK_DEV = 64
CELLS = 64
KSIZE = 21
NBASIS = 9
NSET = 64
PATCHES = 8
CAP = 32
NBLK = 2048
N_PATCH = 8


def draw_owner(key, part):
    hot_patch = jax.random.randint(jax.random.fold_in(key, 11), (), 0, PATCHES).astype(jnp.int32)
    others = ((hot_patch + 1 + jnp.repeat(jnp.arange(PATCHES - 1), CAP)) % PATCHES).astype(jnp.int32)

    def one_device(device_key):
        first_key, second_key = jax.random.split(device_key)
        picked = jax.random.permutation(first_key, others)[:BLK_DEV - CAP]
        listing = jnp.concatenate([jnp.full((CAP,), hot_patch, jnp.int32), picked])
        return jax.random.permutation(second_key, listing)
    device_keys = jax.random.split(jax.random.fold_in(key, 13), NBLK // BLK_DEV)
    return jax.vmap(one_device)(device_keys).reshape(NBLK).astype(jnp.int32)


def draw_mask_bits(key, part):
    rolls = jax.random.randint(key, (NBLK, BP, BP), 0, 2 ** 24)
    bad_bit = (rolls % 64 < 4).astype(jnp.int32)
    saturated = (rolls // 64 % 64 < 2).astype(jnp.int32)
    cosmic_bit = (rolls // 4096 % 64 < 4).astype(jnp.int32)
    interpolated = (rolls // 262144 % 64 < 16).astype(jnp.int32)
    flags = bad_bit + 2 * saturated + 4 * cosmic_bit + 8 * interpolated
    return flags.at[0, 0, 0].set(15).at[0, 0, 1].set(0).astype(jnp.int32)


def plant(values, own_key, low, high):
    extent = values.shape
    spot = [jax.random.randint(jax.random.fold_in(own_key, axis), (), 0, extent[axis]) for axis in range(len(extent))]
    values = values.at[tuple(spot)].set(low)
    longest = extent.index(max(extent))
    spot[longest] = (spot[longest] + 1) % extent[longest]
    return values.at[tuple(spot)].set(high)


def block_scale(key, shape, shards, low, top_value):
    def one(axis_at, blocks):
        heights = jax.random.uniform(jax.random.fold_in(jax.random.fold_in(key, 6), axis_at), (blocks,), jnp.float32, low / len(shards), top_value / len(shards))
        return jnp.repeat(jnp.exp(heights), shape[axis_at] // blocks).reshape((-1,) + (1,) * (len(shape) - axis_at - 1))

    factor_of = one(*shards[0])
    for cut in shards[1:]:
        factor_of = factor_of * one(*cut)
    return factor_of


def normal_values(key, extent, scale, bound, pieces=(), held_as=jnp.bfloat16):
    values = jax.random.normal(key, extent, jnp.float32) * scale
    if len(pieces) > 0:
        values = block_scale(key, extent, pieces, -0.22, 0.18) * values
    return jnp.clip(values, min=-bound, max=bound).astype(held_as)


def setup_inputs(seed: int = 0) -> dict:
    arg_keys = jax.random.split(jax.random.key(seed), 8)
    pixels = normal_values(arg_keys[0], (NBLK, BP, BP), 1.0, 6.0, ((0, 32),))
    mask_bits = draw_mask_bits(jax.random.fold_in(arg_keys[7], 71), 0)
    inv_var = jnp.clip(jnp.exp(math.log(1.0) - 2.9957323 * jax.random.uniform(arg_keys[2], (NBLK,), jnp.float32) ** block_scale(arg_keys[2], (NBLK,), ((0, 32),), -0.2, 0.2)), 0.05, 1.0)
    owner = draw_owner(jax.random.fold_in(arg_keys[7], 71), 0)
    cell = plant(jax.random.randint(arg_keys[4], (NBLK,), 0, CELLS), jax.random.fold_in(arg_keys[4], 1), 0, CELLS - 1).astype(jnp.int32)
    coef_index = plant(jax.random.randint(arg_keys[5], (NBLK,), 0, NSET), jax.random.fold_in(arg_keys[5], 1), 0, NSET - 1).astype(jnp.int32)
    coef_table = normal_values(arg_keys[6], (NSET, NBASIS), 0.7, 4.0, (), jnp.float32)
    return {"pixels": pixels, "mask_bits": mask_bits, "inv_var": inv_var, "owner": owner, "cell": cell, "coef_index": coef_index, "coef_table": coef_table}


gauss_widths = (1.0, 2.0, 3.5)


def band_tables(side_len):
    tap_reach = KSIZE // 2
    position = jnp.arange(side_len).astype(jnp.float32)
    offset = position[:, None] - position[None, :]
    inside = jnp.abs(offset) <= tap_reach
    tap_offsets = jnp.arange(-tap_reach, tap_reach + 1).astype(jnp.float32)
    tables = []
    for spread in gauss_widths:
        profile_sum = jnp.sum(jnp.exp(-tap_offsets * tap_offsets / (2.0 * spread * spread)))
        even_band = jnp.where(inside, jnp.exp(-offset * offset / (2.0 * spread * spread)) / profile_sum, 0.0)
        tables.append(even_band)
        tables.append(even_band * offset / spread)
    return jnp.stack(tables)


def match_group(blocks, coefficients, tables, right_bands):
    number = blocks.shape[0]
    side_len = blocks.shape[1]
    columns = jnp.dot(blocks.reshape(number * side_len, side_len), right_bands, preferred_element_type=jnp.float32)
    columns = columns.astype(jnp.bfloat16).reshape(number, side_len, 6, side_len)
    left_parts = []
    for sigma_pos in range(3):
        even_band = tables[2 * sigma_pos]
        odd_band = tables[2 * sigma_pos + 1]
        left_parts.append(coefficients[:, 3 * sigma_pos, None, None] * even_band + coefficients[:, 3 * sigma_pos + 1, None, None] * odd_band)
        left_parts.append(coefficients[:, 3 * sigma_pos + 2, None, None] * even_band)
    left_bands = jnp.stack(left_parts, axis=2).astype(jnp.bfloat16)
    result = jnp.einsum("nisp,npsj->nij", left_bands.astype(jnp.float32), columns.astype(jnp.float32))
    return result.astype(jnp.bfloat16)


def reference(pixels, mask_bits, inv_var, owner, cell, coef_index, coef_table):
    number = pixels.shape[0]
    side_len = pixels.shape[1]
    tables = band_tables(side_len)
    right_bands = jnp.transpose(tables, (2, 0, 1)).reshape(side_len, 6 * side_len).astype(jnp.bfloat16)
    usable = (mask_bits % 2 == 0) & ((mask_bits // 2) % 2 == 0) & ((mask_bits // 4) % 2 == 0)
    masked = jnp.where(usable, pixels, jnp.zeros((), jnp.bfloat16))
    chosen = (coef_index[:, None] == jnp.arange(NSET).astype(jnp.int32)[None, :]).astype(jnp.float32)
    coefficients = jnp.dot(chosen, coef_table, precision=lax.Precision.HIGHEST)
    rounds = number // 64

    def one_batch(bundle):
        return match_group(bundle[0], bundle[1], tables, right_bands)

    matched = lax.map(one_batch, (masked.reshape(rounds, 64, side_len, side_len), coefficients.reshape(rounds, 64, NBASIS)))
    matched = matched.reshape(number, side_len, side_len)
    weight = lax.optimization_barrier(inv_var.astype(jnp.bfloat16)).astype(jnp.float32)
    segment = (owner * CELLS + cell).astype(jnp.int32)
    numerator = jax.ops.segment_sum(weight[:, None, None] * matched.astype(jnp.float32), segment, num_segments=N_PATCH * CELLS)
    weight_sum = jax.ops.segment_sum(weight, segment, num_segments=N_PATCH * CELLS)
    coadd = numerator / jnp.maximum(weight_sum, 1.0)[:, None, None]
    template = coadd.astype(jnp.bfloat16)
    difference = (matched.astype(jnp.float32) - template[segment].astype(jnp.float32)).astype(jnp.bfloat16)
    return coadd, difference
```

```python
import jax
import jax.numpy as jnp
from jax import lax
from jax.experimental import pallas as pl
from jax.experimental.pallas import tpu as pltpu
from jax.sharding import PartitionSpec as P

CELLS = 64
KSIZE = 21


gauss_widths = (1.0, 2.0, 3.5)


def band_tables(side_len):
    tap_reach = KSIZE // 2
    position = jnp.arange(side_len).astype(jnp.float32)
    offset = position[:, None] - position[None, :]
    inside = jnp.abs(offset) <= tap_reach
    tap_offsets = jnp.arange(-tap_reach, tap_reach + 1).astype(jnp.float32)
    tables = []
    for spread in gauss_widths:
        profile_sum = jnp.sum(jnp.exp(-tap_offsets * tap_offsets / (2.0 * spread * spread)))
        even_band = jnp.where(
            inside, jnp.exp(-offset * offset / (2.0 * spread * spread)) / profile_sum, 0.0
        )
        tables.append(even_band)
        tables.append(even_band * offset / spread)
    return jnp.stack(tables)


def match_group(blocks, coefficients, tables, right_bands):
    number = blocks.shape[0]
    side_len = blocks.shape[1]
    columns = jnp.dot(
        blocks.reshape(number * side_len, side_len), right_bands, preferred_element_type=jnp.float32
    )
    columns = columns.astype(jnp.bfloat16).reshape(number, side_len, 6, side_len)
    left_parts = []
    for sigma_pos in range(3):
        even_band = tables[2 * sigma_pos]
        odd_band = tables[2 * sigma_pos + 1]
        left_parts.append(
            coefficients[:, 3 * sigma_pos, None, None] * even_band
            + coefficients[:, 3 * sigma_pos + 1, None, None] * odd_band
        )
        left_parts.append(coefficients[:, 3 * sigma_pos + 2, None, None] * even_band)
    left_bands = jnp.stack(left_parts, axis=2).astype(jnp.bfloat16)
    result = jnp.einsum("nisp,npsj->nij", left_bands, columns, preferred_element_type=jnp.float32)
    return result.astype(jnp.bfloat16)


def match_blocks(blocks, coefficients, tables, right_bands):
    number = blocks.shape[0]
    side_len = blocks.shape[1]
    batch_blocks = 16
    rounds = -(-number // batch_blocks)

    def one_batch(bundle):
        return match_group(bundle[0], bundle[1], tables, right_bands)

    matched = lax.map(
        one_batch,
        (
            blocks.reshape(rounds, batch_blocks, side_len, side_len),
            coefficients.reshape(rounds, batch_blocks, coefficients.shape[1]),
        ),
    )
    return matched.reshape(rounds * batch_blocks, side_len, side_len)[:number]


def shards(pixels, mask_bits, inv_var, owner, cell, coef_index, coef_table):
    blocks_here = pixels.shape[0]
    side_len = pixels.shape[1]
    kernel_sets = coef_table.shape[0]
    patches = lax.axis_size("patch")
    visits = lax.axis_size("visit")
    capacity = 4 * blocks_here // patches
    slot_total = patches * capacity
    tables = band_tables(side_len)
    right_bands = (
        jnp.transpose(tables, (2, 0, 1)).reshape(side_len, 6 * side_len).astype(jnp.bfloat16)
    )
    usable = (mask_bits % 2 == 0) & (mask_bits // 2 % 2 == 0) & (mask_bits // 4 % 2 == 0)
    masked = jnp.where(usable, pixels, jnp.zeros((), jnp.bfloat16))
    weight = inv_var.astype(jnp.bfloat16)
    cell_weight = jnp.where(
        cell[:, None] == jnp.arange(CELLS)[None, :], weight[:, None], jnp.zeros((), jnp.bfloat16)
    )
    chosen = (coef_index[:, None] == jnp.arange(kernel_sets)[None, :]).astype(jnp.bfloat16)
    dest_onehot = (owner[:, None] == jnp.arange(patches)[None, :]).astype(jnp.int32)
    slot_rank = jnp.sum((jnp.cumsum(dest_onehot, axis=0) - dest_onehot) * dest_onehot, axis=1)
    slot_of_block = owner * capacity + slot_rank
    matches = slot_of_block[None, :] == jnp.arange(slot_total)[:, None]
    source_row = jnp.sum(jnp.where(matches, jnp.arange(blocks_here)[None, :], 0), axis=1)
    filled = jnp.any(matches, axis=1)

    def pack_slots(values):
        picked = values[source_row]
        keep_rows = filled.reshape((slot_total,) + (1,) * (values.ndim - 1))
        picked = jnp.where(keep_rows, picked, jnp.zeros((), values.dtype))
        return picked.reshape((patches, capacity) + values.shape[1:])

    pieces = lax.all_to_all(pack_slots(masked), "patch", split_axis=0, concat_axis=0, tiled=True)
    weights = lax.all_to_all(
        pack_slots(cell_weight), "patch", split_axis=0, concat_axis=0, tiled=True
    )
    kernel_picks = lax.all_to_all(
        pack_slots(chosen), "patch", split_axis=0, concat_axis=0, tiled=True
    )
    flat_blocks = pieces.reshape((-1, side_len, side_len))
    coefficients = jnp.dot(
        kernel_picks.reshape(-1, kernel_sets).astype(jnp.float32),
        coef_table,
        precision=lax.Precision.HIGHEST,
    )
    matched = match_blocks(flat_blocks, coefficients, tables, right_bands)
    matched_slots = matched.reshape(pieces.shape)
    flat_weights = weights.reshape(slot_total, CELLS)
    flat_matched = matched_slots.reshape(slot_total, side_len * side_len)
    numerator = jnp.einsum(
        "sc,sk->ck", flat_weights, flat_matched, preferred_element_type=jnp.float32
    ).reshape(CELLS, side_len, side_len)
    weight_sum = jnp.sum(flat_weights.astype(jnp.float32), axis=0)
    rows_here = side_len // visits
    numerator, weight_sum = lax.psum((numerator, weight_sum), "visit")
    coadd_full = numerator / jnp.maximum(weight_sum, 1.0)[:, None, None]
    coadd_part = lax.dynamic_slice_in_dim(
        coadd_full, lax.axis_index("visit") * rows_here, rows_here, 1
    )
    template = coadd_full.astype(jnp.bfloat16)
    live_slots = (flat_weights > 0).astype(jnp.bfloat16)
    slot_template = jnp.einsum(
        "sc,ck->sk",
        live_slots,
        template.reshape(CELLS, side_len * side_len),
        preferred_element_type=jnp.float32,
    )
    difference_slots = (flat_matched.astype(jnp.float32) - slot_template).astype(jnp.bfloat16)
    returned = lax.all_to_all(
        difference_slots.reshape(patches, capacity, side_len, side_len),
        "patch",
        split_axis=0,
        concat_axis=0,
        tiled=True,
    )
    difference = returned.reshape(slot_total, side_len, side_len)[slot_of_block]
    return (coadd_part, difference)


GROUP = 16
HALF = 4
ROWS = 8
STEPS = 4
PAIR = ROWS // STEPS
MESH = pl.DeviceIdType.MESH


def match_kernel(coef_ref, pixels_ref, mask_ref, right_ref, tables_ref, out_ref, wide):
    step = pl.program_id(0)
    per_step, side_len = pixels_ref.shape[0], pixels_ref.shape[1]
    unit = 4

    def some(part, carry):
        first = part * unit
        usable = (mask_ref[pl.ds(first, unit)] & 7) == 0
        masked = jnp.where(usable, pixels_ref[pl.ds(first, unit)].astype(jnp.float32), 0.0)
        masked = masked.astype(jnp.bfloat16).reshape(unit * side_len, side_len)
        columns = jnp.dot(masked, right_ref[...], preferred_element_type=jnp.float32)
        columns = columns.astype(jnp.bfloat16)
        for n in range(unit):
            block = step * per_step + first + n
            left_parts = []
            for m in range(3):
                even, odd = tables_ref[2 * m], tables_ref[2 * m + 1]
                left_parts.append(
                    (coef_ref[block, 3 * m] * even + coef_ref[block, 3 * m + 1] * odd).astype(jnp.bfloat16)
                )
                left_parts.append((coef_ref[block, 3 * m + 2] * even).astype(jnp.bfloat16))
            left = jnp.concatenate(left_parts, axis=1)
            own = columns[n * side_len : (n + 1) * side_len]
            stacked = jnp.concatenate(
                [own[:, p * side_len : (p + 1) * side_len] for p in range(6)], axis=0
            )
            start = pl.multiple_of((first + n) * side_len, side_len)
            wide[pl.ds(start, side_len), :] = jnp.dot(left, stacked, preferred_element_type=jnp.float32)
        return carry

    lax.fori_loop(0, per_step // unit, some, 0)
    for g in range(GROUP):
        for r in range(ROWS):
            rows = wide[pl.ds(g * ROWS + r, per_step, stride=side_len), :]
            lane = r % PAIR * side_len
            out_ref[r // PAIR, g, :, lane : lane + side_len] = rows.astype(jnp.bfloat16)


def match_rows(pixels, mask_bits, coefficients, right_bands, tables):
    blocks, side_len = pixels.shape[0], pixels.shape[1]
    per_step = 16
    return pl.pallas_call(
        match_kernel,
        grid=(blocks // per_step,),
        in_specs=[
            pl.BlockSpec(memory_space=pltpu.SMEM),
            pl.BlockSpec((per_step, side_len, side_len), lambda i: (i, 0, 0)),
            pl.BlockSpec((per_step, side_len, side_len), lambda i: (i, 0, 0)),
            pl.BlockSpec(right_bands.shape, lambda i: (0, 0)),
            pl.BlockSpec(tables.shape, lambda i: (0, 0, 0)),
        ],
        out_specs=pl.BlockSpec((STEPS, GROUP, per_step, PAIR * side_len), lambda i: (0, 0, i, 0)),
        out_shape=jax.ShapeDtypeStruct((STEPS, GROUP, blocks, PAIR * side_len), jnp.bfloat16),
        scratch_shapes=[pltpu.VMEM((per_step * side_len, side_len), jnp.float32)],
        compiler_params=pltpu.CompilerParams(vmem_limit_bytes=40 * 2**20),
    )(coefficients, pixels, mask_bits, right_bands, tables)


def trade_kernel(
    rows_ref, seg_row_ref, weight_row_ref, seg_column_ref, scale_ref,
    coadd_ref, difference_ref,
    held, sums, sums_out, sums_in, templates, coadd_in, diffs, diffs_in, weights, picks, wide,
    send_rows, recv_rows, send_sums, recv_sums, send_coadd, recv_coadd, send_diffs, recv_diffs,
):
    side_len = wide.shape[1]
    blocks = held.shape[2]
    total = GROUP * blocks
    cells = weights.shape[0]
    visit, patch = lax.axis_index("visit"), lax.axis_index("patch")
    half, place = patch // HALF, patch % HALF
    me = visit * HALF + place

    def device_of(index):
        return (index // HALF, half * HALF + index % HALF)

    partner = (visit, (1 - half) * HALF + place)
    barrier = pltpu.get_barrier_semaphore()

    def peers(act):
        def one(turn, carry):
            act((me + turn) % GROUP)
            return carry

        lax.fori_loop(1, GROUP, one, 0)

    peers(
        lambda peer: pl.semaphore_signal(
            barrier, inc=1, device_id=device_of(peer), device_id_type=MESH
        )
    )
    pl.semaphore_signal(barrier, inc=1, device_id=partner, device_id_type=MESH)
    pl.semaphore_wait(barrier, GROUP)

    def rows_copy(step, peer, slot):
        return pltpu.make_async_remote_copy(
            src_ref=rows_ref.at[step, peer], dst_ref=held.at[step, slot],
            send_sem=send_rows.at[step, peer], recv_sem=recv_rows.at[step, slot],
            device_id=device_of(peer), device_id_type=MESH,
        )

    def sums_copy(step):
        return pltpu.make_async_remote_copy(
            src_ref=sums_out.at[step], dst_ref=sums_in.at[step],
            send_sem=send_sums.at[step], recv_sem=recv_sums.at[step],
            device_id=partner, device_id_type=MESH,
        )

    def coadd_copy(step, peer, slot):
        start = pl.multiple_of((half * HALF + peer) * CELLS, CELLS)
        return pltpu.make_async_remote_copy(
            src_ref=templates.at[step, pl.ds(start, CELLS)], dst_ref=coadd_in.at[step, slot],
            send_sem=send_coadd.at[step, peer], recv_sem=recv_coadd.at[step, slot],
            device_id=(visit, half * HALF + peer), device_id_type=MESH,
        )

    def diffs_copy(step, peer, slot):
        return pltpu.make_async_remote_copy(
            src_ref=diffs.at[step, peer], dst_ref=diffs_in.at[step, slot],
            send_sem=send_diffs.at[step, peer], recv_sem=recv_diffs.at[step, slot],
            device_id=device_of(peer), device_id_type=MESH,
        )

    for step in range(STEPS):
        peers(lambda peer: rows_copy(step, peer, me).start())
        held[step, pl.ds(me, 1)] = rows_ref[step, pl.ds(me, 1)]

    strip = 64

    def make_weights(part, carry):
        start = pl.multiple_of(part * strip, strip)
        cell = lax.broadcasted_iota(jnp.int32, (strip, total), 0) + start
        chosen = jnp.where(cell == seg_row_ref[...], weight_row_ref[...], 0.0)
        weights[pl.ds(start, strip), :] = chosen.astype(jnp.bfloat16)
        return carry

    lax.fori_loop(0, cells // strip, make_weights, 0)

    def make_picks(part, carry):
        start = pl.multiple_of(part * strip, strip)
        cell = lax.broadcasted_iota(jnp.int32, (strip, cells), 1)
        chosen = jnp.where(cell == seg_column_ref[pl.ds(start, strip), :], 1.0, 0.0)
        picks[pl.ds(start, strip), :] = chosen.astype(jnp.bfloat16)
        return carry

    lax.fori_loop(0, total // strip, make_picks, 0)

    for step in range(STEPS):
        peers(lambda peer: rows_copy(step, peer, peer).wait_recv())
        flat = held[step].reshape(total, PAIR * side_len)
        part_sum = jnp.dot(weights[...], flat, preferred_element_type=jnp.float32)
        sums[step] = part_sum
        sums_out[step] = part_sum.astype(jnp.bfloat16)
        sums_copy(step).start()

    for step in range(STEPS):
        sums_copy(step).wait_recv()
        template = (sums[step] + sums_in[step].astype(jnp.float32)) * scale_ref[...]
        templates[step] = template.astype(jnp.bfloat16)
        flat = held[step].reshape(total, PAIR * side_len)
        chosen = jnp.dot(picks[...], templates[step], preferred_element_type=jnp.float32)
        change = (flat.astype(jnp.float32) - chosen).astype(jnp.bfloat16)
        diffs[step] = change.reshape(GROUP, blocks, PAIR * side_len)
        peers(lambda peer: diffs_copy(step, peer, me).start())
        for turn in range(1, HALF):
            coadd_copy(step, (place + turn) % HALF, place).start()
        start = pl.multiple_of(patch * CELLS, CELLS)
        coadd_in[step, pl.ds(place, 1)] = templates[step, pl.ds(start, CELLS)].reshape(
            1, CELLS, PAIR * side_len
        )
        diffs_in[step, pl.ds(me, 1)] = diffs[step, pl.ds(me, 1)]

    rows_here = HALF * ROWS
    for step in range(STEPS):
        peers(lambda peer: diffs_copy(step, peer, peer).wait_recv())

        def spread(source, carry):
            values = diffs_in[step, source].astype(jnp.float32)
            for k in range(PAIR):
                row = source * ROWS + step * PAIR + k
                wide[pl.ds(row, blocks, stride=side_len), :] = values[
                    :, k * side_len : (k + 1) * side_len
                ]
            return carry

        lax.fori_loop(0, GROUP, spread, 0)
        for turn in range(1, HALF):
            peer = (place + turn) % HALF
            coadd_copy(step, peer, peer).wait_recv()
        for source in range(HALF):
            values = coadd_in[step, source].astype(jnp.float32)
            for k in range(PAIR):
                row = source * ROWS + step * PAIR + k
                coadd_ref[pl.ds(row, CELLS, stride=rows_here), :] = values[
                    :, k * side_len : (k + 1) * side_len
                ]

    def narrow(part, carry):
        start = pl.multiple_of(part * 512, 512)
        difference_ref[pl.ds(start, 512), :] = wide[pl.ds(start, 512), :].astype(jnp.bfloat16)
        return carry

    lax.fori_loop(0, wide.shape[0] // 512, narrow, 0)

    for step in range(STEPS):
        peers(lambda peer: rows_copy(step, peer, me).wait_send())
        sums_copy(step).wait_send()
        peers(lambda peer: diffs_copy(step, peer, me).wait_send())
        for turn in range(1, HALF):
            coadd_copy(step, (place + turn) % HALF, place).wait_send()


def trade(rows, seg_row, weight_row, seg_column, scale, side_len):
    blocks, width = rows.shape[2], rows.shape[3]
    total = GROUP * blocks
    cells = scale.shape[0]
    bf16, f32 = jnp.bfloat16, jnp.float32
    dma = pltpu.SemaphoreType.DMA
    return pl.pallas_call(
        trade_kernel,
        in_specs=[pl.BlockSpec(memory_space=pltpu.VMEM)] * 5,
        out_specs=[pl.BlockSpec(memory_space=pltpu.VMEM)] * 2,
        out_shape=[
            jax.ShapeDtypeStruct((CELLS * HALF * ROWS, side_len), f32),
            jax.ShapeDtypeStruct((blocks * side_len, side_len), bf16),
        ],
        scratch_shapes=[
            pltpu.VMEM((STEPS, GROUP, blocks, width), bf16),
            pltpu.VMEM((STEPS, cells, width), f32),
            pltpu.VMEM((STEPS, cells, width), bf16),
            pltpu.VMEM((STEPS, cells, width), bf16),
            pltpu.VMEM((STEPS, cells, width), bf16),
            pltpu.VMEM((STEPS, HALF, CELLS, width), bf16),
            pltpu.VMEM((STEPS, GROUP, blocks, width), bf16),
            pltpu.VMEM((STEPS, GROUP, blocks, width), bf16),
            pltpu.VMEM((cells, total), bf16),
            pltpu.VMEM((total, cells), bf16),
            pltpu.VMEM((blocks * side_len, side_len), f32),
            dma((STEPS, GROUP)),
            dma((STEPS, GROUP)),
            dma((STEPS,)),
            dma((STEPS,)),
            dma((STEPS, HALF)),
            dma((STEPS, HALF)),
            dma((STEPS, GROUP)),
            dma((STEPS, GROUP)),
        ],
        compiler_params=pltpu.CompilerParams(
            collective_id=0, has_side_effects=True, vmem_limit_bytes=48 * 2**20
        ),
    )(rows, seg_row, weight_row, seg_column, scale)


def row_shards(pixels, mask_bits, inv_var, owner, cell, coef_index, coef_table):
    blocks, side_len = pixels.shape[0], pixels.shape[1]
    patches = lax.axis_size("patch")
    visits = lax.axis_size("visit")
    cells = patches * CELLS
    tables = band_tables(side_len)
    right_bands = (
        jnp.transpose(tables, (2, 0, 1)).reshape(side_len, 6 * side_len).astype(jnp.bfloat16)
    )
    weight = inv_var.astype(jnp.bfloat16).astype(jnp.float32)
    segment = (owner * CELLS + cell).astype(jnp.float32)
    facts = lax.all_gather(jnp.stack([segment, weight]), ("visit", "patch"), tiled=False)
    coefficients = coef_table[coef_index]
    rows = match_rows(pixels, mask_bits, coefficients, right_bands, tables)
    every_segment = facts[:, 0].astype(jnp.int32).reshape(1, -1)
    every_weight = facts[:, 1].reshape(1, -1)
    weight_sum = jnp.sum(
        jnp.where(jnp.arange(cells, dtype=jnp.int32)[:, None] == every_segment, every_weight, 0.0), axis=1
    )
    scale = (1.0 / jnp.maximum(weight_sum, 1.0))[:, None]
    half = lax.axis_index("patch") // HALF
    near = lax.dynamic_index_in_dim(
        facts.reshape(visits, patches // HALF, HALF, 2, blocks), half, 1, keepdims=False
    ).reshape(GROUP, 2, blocks)
    near_segment = near[:, 0].astype(jnp.int32)
    coadd, difference = trade(
        rows,
        near_segment.reshape(1, -1),
        near[:, 1].reshape(1, -1),
        near_segment.reshape(-1, 1),
        scale,
        side_len,
    )
    return (
        coadd.reshape(CELLS, HALF * ROWS, side_len),
        difference.reshape(blocks, side_len, side_len),
    )


def solution(mesh):
    placed = (
        P(("visit", "patch"), None, None),
        P(("visit", "patch"), None, None),
        P(("visit", "patch")),
        P(("visit", "patch")),
        P(("visit", "patch")),
        P(("visit", "patch")),
        P(),
    )
    fits = mesh.shape["visit"] == GROUP // HALF and mesh.shape["patch"] == 2 * HALF
    return jax.shard_map(
        row_shards if fits else shards,
        mesh=mesh,
        in_specs=placed,
        out_specs=(P("patch", "visit", None), P(("visit", "patch"), None, None)),
        check_vma=False,
    )
```

```python
import jax
import jax.numpy as jnp
import numpy as np
from jax import lax
from jax.experimental import pallas as pl
from jax.experimental.pallas import tpu as pltpu
from jax.sharding import PartitionSpec as P

CELLS = 64
KSIZE = 21


gauss_widths = (1.0, 2.0, 3.5)


def band_tables(side_len):
    tap_reach = KSIZE // 2
    position = jnp.arange(side_len).astype(jnp.float32)
    offset = position[:, None] - position[None, :]
    inside = jnp.abs(offset) <= tap_reach
    tap_offsets = jnp.arange(-tap_reach, tap_reach + 1).astype(jnp.float32)
    tables = []
    for spread in gauss_widths:
        profile_sum = jnp.sum(jnp.exp(-tap_offsets * tap_offsets / (2.0 * spread * spread)))
        even_band = jnp.where(
            inside, jnp.exp(-offset * offset / (2.0 * spread * spread)) / profile_sum, 0.0
        )
        tables.append(even_band)
        tables.append(even_band * offset / spread)
    return jnp.stack(tables)


def match_group(blocks, coefficients, tables, right_bands):
    number = blocks.shape[0]
    side_len = blocks.shape[1]
    columns = jnp.dot(
        blocks.reshape(number * side_len, side_len), right_bands, preferred_element_type=jnp.float32
    )
    columns = columns.astype(jnp.bfloat16).reshape(number, side_len, 6, side_len)
    left_parts = []
    for sigma_pos in range(3):
        even_band = tables[2 * sigma_pos]
        odd_band = tables[2 * sigma_pos + 1]
        left_parts.append(
            coefficients[:, 3 * sigma_pos, None, None] * even_band
            + coefficients[:, 3 * sigma_pos + 1, None, None] * odd_band
        )
        left_parts.append(coefficients[:, 3 * sigma_pos + 2, None, None] * even_band)
    left_bands = jnp.stack(left_parts, axis=2).astype(jnp.bfloat16)
    result = jnp.einsum("nisp,npsj->nij", left_bands, columns, preferred_element_type=jnp.float32)
    return result.astype(jnp.bfloat16)


def match_blocks(blocks, coefficients, tables, right_bands):
    number = blocks.shape[0]
    side_len = blocks.shape[1]
    batch_blocks = 16
    rounds = -(-number // batch_blocks)

    def one_batch(bundle):
        return match_group(bundle[0], bundle[1], tables, right_bands)

    matched = lax.map(
        one_batch,
        (
            blocks.reshape(rounds, batch_blocks, side_len, side_len),
            coefficients.reshape(rounds, batch_blocks, coefficients.shape[1]),
        ),
    )
    return matched.reshape(rounds * batch_blocks, side_len, side_len)[:number]


def shards(pixels, mask_bits, inv_var, owner, cell, coef_index, coef_table):
    blocks_here = pixels.shape[0]
    side_len = pixels.shape[1]
    kernel_sets = coef_table.shape[0]
    patches = lax.axis_size("patch")
    visits = lax.axis_size("visit")
    capacity = 4 * blocks_here // patches
    slot_total = patches * capacity
    tables = band_tables(side_len)
    right_bands = (
        jnp.transpose(tables, (2, 0, 1)).reshape(side_len, 6 * side_len).astype(jnp.bfloat16)
    )
    usable = (mask_bits % 2 == 0) & (mask_bits // 2 % 2 == 0) & (mask_bits // 4 % 2 == 0)
    masked = jnp.where(usable, pixels, jnp.zeros((), jnp.bfloat16))
    weight = inv_var.astype(jnp.bfloat16)
    cell_weight = jnp.where(
        cell[:, None] == jnp.arange(CELLS)[None, :], weight[:, None], jnp.zeros((), jnp.bfloat16)
    )
    chosen = (coef_index[:, None] == jnp.arange(kernel_sets)[None, :]).astype(jnp.bfloat16)
    dest_onehot = (owner[:, None] == jnp.arange(patches)[None, :]).astype(jnp.int32)
    slot_rank = jnp.sum((jnp.cumsum(dest_onehot, axis=0) - dest_onehot) * dest_onehot, axis=1)
    slot_of_block = owner * capacity + slot_rank
    matches = slot_of_block[None, :] == jnp.arange(slot_total)[:, None]
    source_row = jnp.sum(jnp.where(matches, jnp.arange(blocks_here)[None, :], 0), axis=1)
    filled = jnp.any(matches, axis=1)

    def pack_slots(values):
        picked = values[source_row]
        keep_rows = filled.reshape((slot_total,) + (1,) * (values.ndim - 1))
        picked = jnp.where(keep_rows, picked, jnp.zeros((), values.dtype))
        return picked.reshape((patches, capacity) + values.shape[1:])

    pieces = lax.all_to_all(pack_slots(masked), "patch", split_axis=0, concat_axis=0, tiled=True)
    weights = lax.all_to_all(
        pack_slots(cell_weight), "patch", split_axis=0, concat_axis=0, tiled=True
    )
    kernel_picks = lax.all_to_all(
        pack_slots(chosen), "patch", split_axis=0, concat_axis=0, tiled=True
    )
    flat_blocks = pieces.reshape((-1, side_len, side_len))
    coefficients = jnp.dot(
        kernel_picks.reshape(-1, kernel_sets).astype(jnp.float32),
        coef_table,
        precision=lax.Precision.HIGHEST,
    )
    matched = match_blocks(flat_blocks, coefficients, tables, right_bands)
    matched_slots = matched.reshape(pieces.shape)
    flat_weights = weights.reshape(slot_total, CELLS)
    flat_matched = matched_slots.reshape(slot_total, side_len * side_len)
    numerator = jnp.einsum(
        "sc,sk->ck", flat_weights, flat_matched, preferred_element_type=jnp.float32
    ).reshape(CELLS, side_len, side_len)
    weight_sum = jnp.sum(flat_weights.astype(jnp.float32), axis=0)
    rows_here = side_len // visits
    numerator, weight_sum = lax.psum((numerator, weight_sum), "visit")
    coadd_full = numerator / jnp.maximum(weight_sum, 1.0)[:, None, None]
    coadd_part = lax.dynamic_slice_in_dim(
        coadd_full, lax.axis_index("visit") * rows_here, rows_here, 1
    )
    template = coadd_full.astype(jnp.bfloat16)
    live_slots = (flat_weights > 0).astype(jnp.bfloat16)
    slot_template = jnp.einsum(
        "sc,ck->sk",
        live_slots,
        template.reshape(CELLS, side_len * side_len),
        preferred_element_type=jnp.float32,
    )
    difference_slots = (flat_matched.astype(jnp.float32) - slot_template).astype(jnp.bfloat16)
    returned = lax.all_to_all(
        difference_slots.reshape(patches, capacity, side_len, side_len),
        "patch",
        split_axis=0,
        concat_axis=0,
        tiled=True,
    )
    difference = returned.reshape(slot_total, side_len, side_len)[slot_of_block]
    return (coadd_part, difference)


GROUP = 16
HALF = 4
ROWS = 8
STEPS = 4
PAIR = ROWS // STEPS
MESH = pl.DeviceIdType.MESH


def fixed_bands(side_len):
    reach = KSIZE // 2
    position = np.arange(side_len, dtype=np.float32)
    offset = position[:, None] - position[None, :]
    taps = np.arange(-reach, reach + 1).astype(np.float32)
    tables = []
    for spread in gauss_widths:
        spread = np.float32(spread)
        total = np.sum(np.exp(-taps * taps / (2 * spread * spread)))
        even = np.where(np.abs(offset) <= reach, np.exp(-offset * offset / (2 * spread * spread)) / total, 0)
        tables.append(even.astype(np.float32))
        tables.append((even * offset / spread).astype(np.float32))
    return np.stack(tables)


def trade_kernel(
    index_ref, table_ref, pixels_ref, mask_ref, facts_ref, right_ref, bands_ref,
    coadd_ref, difference_ref,
    rows, held, sums, sums_out, sums_in, templates, coadd_in, diffs, diffs_in, weights, picks, wide,
    facts_in, weight_rows, total_out, total_in, scale,
    send_early, recv_early, send_rows, recv_rows, send_facts, recv_facts, send_total, recv_total,
    send_sums, recv_sums, send_coadd, recv_coadd, send_diffs, recv_diffs,
):
    blocks, side_len = pixels_ref.shape[0], pixels_ref.shape[1]
    total = GROUP * blocks
    early = blocks // 2
    cells = weights.shape[0]
    visit, patch = lax.axis_index("visit"), lax.axis_index("patch")
    half, place = patch // HALF, patch % HALF
    me = visit * HALF + place

    def device_of(index):
        return (index // HALF, half * HALF + index % HALF)

    partner = (visit, (1 - half) * HALF + place)
    barrier = pltpu.get_barrier_semaphore()

    def peers(act):
        def one(turn, carry):
            act((me + turn) % GROUP)
            return carry

        lax.fori_loop(1, GROUP, one, 0)

    peers(
        lambda peer: pl.semaphore_signal(
            barrier, inc=1, device_id=device_of(peer), device_id_type=MESH
        )
    )
    pl.semaphore_signal(barrier, inc=1, device_id=partner, device_id_type=MESH)

    def facts_copy(peer, slot):
        return pltpu.make_async_remote_copy(
            src_ref=facts_ref, dst_ref=facts_in.at[slot],
            send_sem=send_facts.at[peer], recv_sem=recv_facts.at[slot],
            device_id=device_of(peer), device_id_type=MESH,
        )

    def early_copy(peer, slot):
        return pltpu.make_async_remote_copy(
            src_ref=rows.at[:, peer, pl.ds(0, early)], dst_ref=held.at[:, slot, pl.ds(0, early)],
            send_sem=send_early.at[peer], recv_sem=recv_early.at[slot],
            device_id=device_of(peer), device_id_type=MESH,
        )

    def rows_copy(step, peer, slot):
        return pltpu.make_async_remote_copy(
            src_ref=rows.at[step, peer, pl.ds(early, blocks - early)],
            dst_ref=held.at[step, slot, pl.ds(early, blocks - early)],
            send_sem=send_rows.at[step, peer], recv_sem=recv_rows.at[step, slot],
            device_id=device_of(peer), device_id_type=MESH,
        )

    def total_copy():
        return pltpu.make_async_remote_copy(
            src_ref=total_out, dst_ref=total_in, send_sem=send_total, recv_sem=recv_total,
            device_id=partner, device_id_type=MESH,
        )

    def sums_copy(step):
        return pltpu.make_async_remote_copy(
            src_ref=sums_out.at[step], dst_ref=sums_in.at[step],
            send_sem=send_sums.at[step], recv_sem=recv_sums.at[step],
            device_id=partner, device_id_type=MESH,
        )

    def coadd_copy(step, peer, slot):
        start = pl.multiple_of((half * HALF + peer) * CELLS, CELLS)
        return pltpu.make_async_remote_copy(
            src_ref=templates.at[step, pl.ds(start, CELLS)], dst_ref=coadd_in.at[step, slot],
            send_sem=send_coadd.at[step, peer], recv_sem=recv_coadd.at[step, slot],
            device_id=(visit, half * HALF + peer), device_id_type=MESH,
        )

    def diffs_copy(step, peer, slot):
        return pltpu.make_async_remote_copy(
            src_ref=diffs.at[step, peer], dst_ref=diffs_in.at[step, slot],
            send_sem=send_diffs.at[step, peer], recv_sem=recv_diffs.at[step, slot],
            device_id=device_of(peer), device_id_type=MESH,
        )

    unit = 4

    def match_unit(part, carry):
        first = part * unit
        usable = (mask_ref[pl.ds(first, unit)] & 7) == 0
        masked = jnp.where(usable, pixels_ref[pl.ds(first, unit)].astype(jnp.float32), 0.0)
        masked = masked.astype(jnp.bfloat16).reshape(unit * side_len, side_len)
        columns = jnp.dot(masked, right_ref[...], preferred_element_type=jnp.float32)
        columns = columns.astype(jnp.bfloat16)
        for n in range(unit):
            kernel_set = index_ref[first + n]
            left_parts = []
            for m in range(3):
                even, odd = bands_ref[2 * m], bands_ref[2 * m + 1]
                coef = [table_ref[kernel_set, 3 * m + t] for t in range(3)]
                left_parts.append((coef[0] * even + coef[1] * odd).astype(jnp.bfloat16))
                left_parts.append((coef[2] * even).astype(jnp.bfloat16))
            left = jnp.concatenate(left_parts, axis=1)
            own = columns[n * side_len : (n + 1) * side_len]
            stacked = jnp.concatenate(
                [own[:, p * side_len : (p + 1) * side_len] for p in range(6)], axis=0
            )
            start = pl.multiple_of((first + n) * side_len, side_len)
            wide[pl.ds(start, side_len), :] = jnp.dot(left, stacked, preferred_element_type=jnp.float32)
        return carry

    def match_part(first, number):
        lax.fori_loop(first // unit, (first + number) // unit, match_unit, 0)

        def gather_rows(g, carry):
            for r in range(ROWS):
                start = first * side_len + g * ROWS + r
                values = wide[pl.ds(start, number, stride=side_len), :].astype(jnp.bfloat16)
                lane = r % PAIR * side_len
                rows[r // PAIR, g, pl.ds(first, number), lane : lane + side_len] = values
            return carry

        lax.fori_loop(0, GROUP, gather_rows, 0)

    match_part(0, early)
    pl.semaphore_wait(barrier, GROUP)
    peers(lambda peer: facts_copy(peer, me).start())
    peers(lambda peer: early_copy(peer, me).start())
    match_part(early, blocks - early)
    for step in range(STEPS):
        peers(lambda peer: rows_copy(step, peer, me).start())
        held[step, pl.ds(me, 1)] = rows[step, pl.ds(me, 1)]

    facts_in[pl.ds(me, 1)] = facts_ref[...].reshape((1,) + facts_ref.shape)
    peers(lambda peer: facts_copy(peer, peer).wait_recv())
    lanes = 2 * blocks

    def make_pickers(pair, carry):
        first_lanes = lax.broadcasted_iota(jnp.int32, (1, lanes), 1) < blocks
        segment = jnp.where(first_lanes, facts_in[2 * pair, 0:1, :], facts_in[2 * pair + 1, 0:1, :])
        weight = jnp.where(first_lanes, facts_in[2 * pair, 1:2, :], facts_in[2 * pair + 1, 1:2, :])
        start = pl.multiple_of(pair * lanes, lanes)
        cell = lax.broadcasted_iota(jnp.int32, (cells, lanes), 0).astype(jnp.float32)
        weights[:, pl.ds(start, lanes)] = jnp.where(cell == segment, weight, 0.0).astype(jnp.bfloat16)
        weight_rows[:, pl.ds(start, lanes)] = jnp.broadcast_to(weight, (16, lanes)).astype(jnp.bfloat16)
        segment_column = jnp.broadcast_to(segment, (lanes, lanes)).T
        for c in range(cells // lanes):
            cell = lax.broadcasted_iota(jnp.int32, (lanes, lanes), 1) + c * lanes
            chosen = jnp.where(cell.astype(jnp.float32) == segment_column, 1.0, 0.0)
            picks[pl.ds(start, lanes), c * lanes : (c + 1) * lanes] = chosen.astype(jnp.bfloat16)
        return carry

    lax.fori_loop(0, GROUP // 2, make_pickers, 0)
    part_total = jnp.dot(weight_rows[...], picks[...], preferred_element_type=jnp.float32)
    total_out[...] = part_total[0:8]
    total_copy().start()
    peers(lambda peer: early_copy(peer, peer).wait_recv())

    for step in range(STEPS):
        peers(lambda peer: rows_copy(step, peer, peer).wait_recv())
        flat = held[step].reshape(total, PAIR * side_len)
        part_sum = jnp.dot(weights[...], flat, preferred_element_type=jnp.float32)
        sums[step] = part_sum
        sums_out[step] = part_sum.astype(jnp.bfloat16)
        sums_copy(step).start()

    total_copy().wait_recv()
    scale_row = 1.0 / jnp.maximum(total_out[0:1] + total_in[0:1], 1.0)
    for c in range(cells // lanes):
        scale[c * lanes : (c + 1) * lanes] = jnp.broadcast_to(
            scale_row[:, c * lanes : (c + 1) * lanes], (lanes, lanes)
        ).T

    for step in range(STEPS):
        sums_copy(step).wait_recv()
        whole_sum = sums[step] + sums_in[step].astype(jnp.float32)
        for k in range(PAIR):
            lane = slice(k * side_len, (k + 1) * side_len)
            templates[step, :, lane] = (whole_sum[:, lane] * scale[...]).astype(jnp.bfloat16)
        flat = held[step].reshape(total, PAIR * side_len)
        chosen = jnp.dot(picks[...], templates[step], preferred_element_type=jnp.float32)
        change = (flat.astype(jnp.float32) - chosen).astype(jnp.bfloat16)
        diffs[step] = change.reshape(GROUP, blocks, PAIR * side_len)
        peers(lambda peer: diffs_copy(step, peer, me).start())
        for turn in range(1, HALF):
            coadd_copy(step, (place + turn) % HALF, place).start()
        start = pl.multiple_of(patch * CELLS, CELLS)
        coadd_in[step, pl.ds(place, 1)] = templates[step, pl.ds(start, CELLS)].reshape(
            1, CELLS, PAIR * side_len
        )
        diffs_in[step, pl.ds(me, 1)] = diffs[step, pl.ds(me, 1)]

    rows_here = HALF * ROWS
    for step in range(STEPS):
        peers(lambda peer: diffs_copy(step, peer, peer).wait_recv())

        def spread(source, carry):
            values = diffs_in[step, source].astype(jnp.float32)
            for k in range(PAIR):
                row = source * ROWS + step * PAIR + k
                wide[pl.ds(row, blocks, stride=side_len), :] = values[
                    :, k * side_len : (k + 1) * side_len
                ]
            return carry

        lax.fori_loop(0, GROUP, spread, 0)
        for turn in range(1, HALF):
            peer = (place + turn) % HALF
            coadd_copy(step, peer, peer).wait_recv()
        for source in range(HALF):
            values = coadd_in[step, source].astype(jnp.float32)
            for k in range(PAIR):
                row = source * ROWS + step * PAIR + k
                coadd_ref[pl.ds(row, CELLS, stride=rows_here), :] = values[
                    :, k * side_len : (k + 1) * side_len
                ]

    def narrow(part, carry):
        start = pl.multiple_of(part * 512, 512)
        difference_ref[pl.ds(start, 512), :] = wide[pl.ds(start, 512), :].astype(jnp.bfloat16)
        return carry

    lax.fori_loop(0, wide.shape[0] // 512, narrow, 0)

    peers(lambda peer: facts_copy(peer, me).wait_send())
    peers(lambda peer: early_copy(peer, me).wait_send())
    total_copy().wait_send()
    for step in range(STEPS):
        peers(lambda peer: rows_copy(step, peer, me).wait_send())
        sums_copy(step).wait_send()
        peers(lambda peer: diffs_copy(step, peer, me).wait_send())
        for turn in range(1, HALF):
            coadd_copy(step, (place + turn) % HALF, place).wait_send()


def row_shards(pixels, mask_bits, inv_var, owner, cell, coef_index, coef_table):
    blocks, side_len = pixels.shape[0], pixels.shape[1]
    cells = lax.axis_size("patch") * CELLS
    total = GROUP * blocks
    width = PAIR * side_len
    bands = fixed_bands(side_len)
    right_bands = np.transpose(bands, (2, 0, 1)).reshape(side_len, 6 * side_len)
    weight = inv_var.astype(jnp.bfloat16).astype(jnp.float32)
    segment = (owner * CELLS + cell).astype(jnp.float32)
    facts = jnp.pad(jnp.tile(jnp.stack([segment, weight]), (1, 2)), ((0, 6), (0, 0)))
    bf16, f32 = jnp.bfloat16, jnp.float32
    dma = pltpu.SemaphoreType.DMA
    coadd, difference = pl.pallas_call(
        trade_kernel,
        in_specs=[pl.BlockSpec(memory_space=pltpu.SMEM)] * 2
        + [pl.BlockSpec(memory_space=pltpu.VMEM)] * 5,
        out_specs=[pl.BlockSpec(memory_space=pltpu.VMEM)] * 2,
        out_shape=[
            jax.ShapeDtypeStruct((CELLS * HALF * ROWS, side_len), f32),
            jax.ShapeDtypeStruct((blocks * side_len, side_len), bf16),
        ],
        scratch_shapes=[
            pltpu.VMEM((STEPS, GROUP, blocks, width), bf16),
            pltpu.VMEM((STEPS, GROUP, blocks, width), bf16),
            pltpu.VMEM((STEPS, cells, width), f32),
            pltpu.VMEM((STEPS, cells, width), bf16),
            pltpu.VMEM((STEPS, cells, width), bf16),
            pltpu.VMEM((STEPS, cells, width), bf16),
            pltpu.VMEM((STEPS, HALF, CELLS, width), bf16),
            pltpu.VMEM((STEPS, GROUP, blocks, width), bf16),
            pltpu.VMEM((STEPS, GROUP, blocks, width), bf16),
            pltpu.VMEM((cells, total), bf16),
            pltpu.VMEM((total, cells), bf16),
            pltpu.VMEM((blocks * side_len, side_len), f32),
            pltpu.VMEM((GROUP, 8, 2 * blocks), f32),
            pltpu.VMEM((16, total), bf16),
            pltpu.VMEM((8, cells), f32),
            pltpu.VMEM((8, cells), f32),
            pltpu.VMEM((cells, side_len), f32),
            dma((GROUP,)),
            dma((GROUP,)),
            dma((STEPS, GROUP)),
            dma((STEPS, GROUP)),
            dma((GROUP,)),
            dma((GROUP,)),
            dma,
            dma,
            dma((STEPS,)),
            dma((STEPS,)),
            dma((STEPS, HALF)),
            dma((STEPS, HALF)),
            dma((STEPS, GROUP)),
            dma((STEPS, GROUP)),
        ],
        compiler_params=pltpu.CompilerParams(
            collective_id=0, has_side_effects=True, vmem_limit_bytes=56 * 2**20
        ),
    )(
        coef_index, coef_table, pixels, mask_bits, facts,
        jnp.asarray(right_bands, dtype=bf16), jnp.asarray(bands),
    )
    return (
        coadd.reshape(CELLS, HALF * ROWS, side_len),
        difference.reshape(blocks, side_len, side_len),
    )


def solution(mesh):
    placed = (
        P(("visit", "patch"), None, None),
        P(("visit", "patch"), None, None),
        P(("visit", "patch")),
        P(("visit", "patch")),
        P(("visit", "patch")),
        P(("visit", "patch")),
        P(),
    )
    fits = mesh.shape["visit"] == GROUP // HALF and mesh.shape["patch"] == 2 * HALF
    return jax.shard_map(
        row_shards if fits else shards,
        mesh=mesh,
        in_specs=placed,
        out_specs=(P("patch", "visit", None), P(("visit", "patch"), None, None)),
        check_vma=False,
    )
```

```python
import jax
import jax.numpy as jnp
import numpy as np
from jax import lax
from jax.experimental import pallas as pl
from jax.experimental.pallas import tpu as pltpu
from jax.sharding import PartitionSpec as P

CELLS = 64
KSIZE = 21


gauss_widths = (1.0, 2.0, 3.5)


def band_tables(side_len):
    tap_reach = KSIZE // 2
    position = jnp.arange(side_len).astype(jnp.float32)
    offset = position[:, None] - position[None, :]
    inside = jnp.abs(offset) <= tap_reach
    tap_offsets = jnp.arange(-tap_reach, tap_reach + 1).astype(jnp.float32)
    tables = []
    for spread in gauss_widths:
        profile_sum = jnp.sum(jnp.exp(-tap_offsets * tap_offsets / (2.0 * spread * spread)))
        even_band = jnp.where(
            inside, jnp.exp(-offset * offset / (2.0 * spread * spread)) / profile_sum, 0.0
        )
        tables.append(even_band)
        tables.append(even_band * offset / spread)
    return jnp.stack(tables)


def match_group(blocks, coefficients, tables, right_bands):
    number = blocks.shape[0]
    side_len = blocks.shape[1]
    columns = jnp.dot(
        blocks.reshape(number * side_len, side_len), right_bands, preferred_element_type=jnp.float32
    )
    columns = columns.astype(jnp.bfloat16).reshape(number, side_len, 6, side_len)
    left_parts = []
    for sigma_pos in range(3):
        even_band = tables[2 * sigma_pos]
        odd_band = tables[2 * sigma_pos + 1]
        left_parts.append(
            coefficients[:, 3 * sigma_pos, None, None] * even_band
            + coefficients[:, 3 * sigma_pos + 1, None, None] * odd_band
        )
        left_parts.append(coefficients[:, 3 * sigma_pos + 2, None, None] * even_band)
    left_bands = jnp.stack(left_parts, axis=2).astype(jnp.bfloat16)
    result = jnp.einsum("nisp,npsj->nij", left_bands, columns, preferred_element_type=jnp.float32)
    return result.astype(jnp.bfloat16)


def match_blocks(blocks, coefficients, tables, right_bands):
    number = blocks.shape[0]
    side_len = blocks.shape[1]
    batch_blocks = 16
    rounds = -(-number // batch_blocks)

    def one_batch(bundle):
        return match_group(bundle[0], bundle[1], tables, right_bands)

    matched = lax.map(
        one_batch,
        (
            blocks.reshape(rounds, batch_blocks, side_len, side_len),
            coefficients.reshape(rounds, batch_blocks, coefficients.shape[1]),
        ),
    )
    return matched.reshape(rounds * batch_blocks, side_len, side_len)[:number]


def shards(pixels, mask_bits, inv_var, owner, cell, coef_index, coef_table):
    blocks_here = pixels.shape[0]
    side_len = pixels.shape[1]
    kernel_sets = coef_table.shape[0]
    patches = lax.axis_size("patch")
    visits = lax.axis_size("visit")
    capacity = 4 * blocks_here // patches
    slot_total = patches * capacity
    tables = band_tables(side_len)
    right_bands = (
        jnp.transpose(tables, (2, 0, 1)).reshape(side_len, 6 * side_len).astype(jnp.bfloat16)
    )
    usable = (mask_bits % 2 == 0) & (mask_bits // 2 % 2 == 0) & (mask_bits // 4 % 2 == 0)
    masked = jnp.where(usable, pixels, jnp.zeros((), jnp.bfloat16))
    weight = inv_var.astype(jnp.bfloat16)
    cell_weight = jnp.where(
        cell[:, None] == jnp.arange(CELLS)[None, :], weight[:, None], jnp.zeros((), jnp.bfloat16)
    )
    chosen = (coef_index[:, None] == jnp.arange(kernel_sets)[None, :]).astype(jnp.bfloat16)
    dest_onehot = (owner[:, None] == jnp.arange(patches)[None, :]).astype(jnp.int32)
    slot_rank = jnp.sum((jnp.cumsum(dest_onehot, axis=0) - dest_onehot) * dest_onehot, axis=1)
    slot_of_block = owner * capacity + slot_rank
    matches = slot_of_block[None, :] == jnp.arange(slot_total)[:, None]
    source_row = jnp.sum(jnp.where(matches, jnp.arange(blocks_here)[None, :], 0), axis=1)
    filled = jnp.any(matches, axis=1)

    def pack_slots(values):
        picked = values[source_row]
        keep_rows = filled.reshape((slot_total,) + (1,) * (values.ndim - 1))
        picked = jnp.where(keep_rows, picked, jnp.zeros((), values.dtype))
        return picked.reshape((patches, capacity) + values.shape[1:])

    pieces = lax.all_to_all(pack_slots(masked), "patch", split_axis=0, concat_axis=0, tiled=True)
    weights = lax.all_to_all(
        pack_slots(cell_weight), "patch", split_axis=0, concat_axis=0, tiled=True
    )
    kernel_picks = lax.all_to_all(
        pack_slots(chosen), "patch", split_axis=0, concat_axis=0, tiled=True
    )
    flat_blocks = pieces.reshape((-1, side_len, side_len))
    coefficients = jnp.dot(
        kernel_picks.reshape(-1, kernel_sets).astype(jnp.float32),
        coef_table,
        precision=lax.Precision.HIGHEST,
    )
    matched = match_blocks(flat_blocks, coefficients, tables, right_bands)
    matched_slots = matched.reshape(pieces.shape)
    flat_weights = weights.reshape(slot_total, CELLS)
    flat_matched = matched_slots.reshape(slot_total, side_len * side_len)
    numerator = jnp.einsum(
        "sc,sk->ck", flat_weights, flat_matched, preferred_element_type=jnp.float32
    ).reshape(CELLS, side_len, side_len)
    weight_sum = jnp.sum(flat_weights.astype(jnp.float32), axis=0)
    rows_here = side_len // visits
    numerator, weight_sum = lax.psum((numerator, weight_sum), "visit")
    coadd_full = numerator / jnp.maximum(weight_sum, 1.0)[:, None, None]
    coadd_part = lax.dynamic_slice_in_dim(
        coadd_full, lax.axis_index("visit") * rows_here, rows_here, 1
    )
    template = coadd_full.astype(jnp.bfloat16)
    live_slots = (flat_weights > 0).astype(jnp.bfloat16)
    slot_template = jnp.einsum(
        "sc,ck->sk",
        live_slots,
        template.reshape(CELLS, side_len * side_len),
        preferred_element_type=jnp.float32,
    )
    difference_slots = (flat_matched.astype(jnp.float32) - slot_template).astype(jnp.bfloat16)
    returned = lax.all_to_all(
        difference_slots.reshape(patches, capacity, side_len, side_len),
        "patch",
        split_axis=0,
        concat_axis=0,
        tiled=True,
    )
    difference = returned.reshape(slot_total, side_len, side_len)[slot_of_block]
    return (coadd_part, difference)


GROUP = 16
HALF = 4
CORES = 2
ADDERS = 8
ROWS = 16
STEPS = 8
PAIR = ROWS // STEPS
LOADS = 4
MESH = pl.DeviceIdType.MESH


def fixed_bands(side_len):
    reach = KSIZE // 2
    position = np.arange(side_len, dtype=np.float32)
    offset = position[:, None] - position[None, :]
    taps = np.arange(-reach, reach + 1).astype(np.float32)
    tables = []
    for spread in gauss_widths:
        spread = np.float32(spread)
        total = np.sum(np.exp(-taps * taps / (2 * spread * spread)))
        even = np.where(np.abs(offset) <= reach, np.exp(-offset * offset / (2 * spread * spread)) / total, 0)
        tables.append(even.astype(np.float32))
        tables.append((even * offset / spread).astype(np.float32))
    return np.stack(tables)


def trade_kernel(
    index_ref, table_ref, inv_var_ref, owner_ref, cell_ref, right_ref, bands_ref, pixels_hbm, mask_hbm,
    coadd_ref, difference_ref,
    pixels, mask, rows, held, sums, sums_out, sums_in, templates, coadd_in, diffs, diffs_in,
    weights, picks, wide, facts, facts_in, weight_rows, total_out, total_in, scale,
    load_pixels, load_mask, send_rows, recv_rows, send_facts, recv_facts, send_total, recv_total,
    send_sums, recv_sums, send_coadd, recv_coadd, send_diffs, recv_diffs,
):
    blocks, side_len = pixels.shape[0], pixels.shape[1]
    total = GROUP * blocks
    cells = weights.shape[0]
    width = PAIR * side_len
    lanes = 2 * blocks
    load = blocks // LOADS
    visit, patch = lax.axis_index("visit"), lax.axis_index("patch")
    half, place, core = patch // HALF, patch % HALF, patch % CORES
    me = visit * HALF + place
    adder = visit * CORES + core
    adds = patch // CORES == 1 + half
    skip_self = jnp.where(adds, 1, 0)

    def device_of(index):
        return (index // HALF, half * HALF + index % HALF)

    def adder_of(index):
        return (index // CORES, (1 + half) * CORES + index % CORES)

    partner = (visit, (2 - half) * CORES + core)
    barrier = pltpu.get_barrier_semaphore()

    def peers(act):
        def one(turn, carry):
            act((me + turn) % GROUP)
            return carry

        lax.fori_loop(1, GROUP, one, 0)

    def adders(act):
        def one(turn, carry):
            act((adder + turn) % ADDERS)
            return carry

        lax.fori_loop(skip_self, ADDERS, one, 0)

    def places(act):
        def one(turn, carry):
            act((place + turn) % HALF)
            return carry

        lax.fori_loop(1, HALF, one, 0)

    def greet(device):
        pl.semaphore_signal(barrier, inc=1, device_id=device, device_id_type=MESH)

    def load_copies(part):
        span = pl.ds(part * load, load)
        return (
            pltpu.make_async_copy(pixels_hbm.at[span], pixels.at[span], load_pixels.at[part]),
            pltpu.make_async_copy(mask_hbm.at[span], mask.at[span], load_mask.at[part]),
        )

    def facts_copy(target, slot):
        return pltpu.make_async_remote_copy(
            src_ref=facts, dst_ref=facts_in.at[slot],
            send_sem=send_facts.at[target], recv_sem=recv_facts.at[slot],
            device_id=adder_of(target), device_id_type=MESH,
        )

    def rows_copy(step, target, slot):
        return pltpu.make_async_remote_copy(
            src_ref=rows.at[step, target], dst_ref=held.at[step, slot],
            send_sem=send_rows.at[step, target], recv_sem=recv_rows.at[step, slot],
            device_id=adder_of(target), device_id_type=MESH,
        )

    def total_copy():
        return pltpu.make_async_remote_copy(
            src_ref=total_out, dst_ref=total_in, send_sem=send_total, recv_sem=recv_total,
            device_id=partner, device_id_type=MESH,
        )

    def sums_copy(step):
        return pltpu.make_async_remote_copy(
            src_ref=sums_out.at[step], dst_ref=sums_in.at[step],
            send_sem=send_sums.at[step], recv_sem=recv_sums.at[step],
            device_id=partner, device_id_type=MESH,
        )

    def coadd_copy(step, peer, slot):
        start = pl.multiple_of((half * HALF + peer) * CELLS, CELLS)
        return pltpu.make_async_remote_copy(
            src_ref=templates.at[step, pl.ds(start, CELLS)], dst_ref=coadd_in.at[step, slot],
            send_sem=send_coadd.at[step, peer], recv_sem=recv_coadd.at[step, slot],
            device_id=(visit, half * HALF + peer), device_id_type=MESH,
        )

    def diffs_copy(step, peer, slot):
        return pltpu.make_async_remote_copy(
            src_ref=diffs.at[step, peer], dst_ref=diffs_in.at[step, slot],
            send_sem=send_diffs.at[step, peer], recv_sem=recv_diffs.at[step, slot],
            device_id=device_of(peer), device_id_type=MESH,
        )

    for part in range(LOADS):
        for copy in load_copies(part):
            copy.start()

    @pl.when(adds)
    def _():
        peers(lambda peer: greet(device_of(peer)))
        greet(partner)

    @pl.when(jnp.logical_not(adds))
    def _():
        adders(lambda target: greet(adder_of(target)))

    segment = (owner_ref[...] * CELLS + cell_ref[...]).astype(jnp.float32)
    weight = inv_var_ref[...].astype(jnp.bfloat16).astype(jnp.float32)
    facts[...] = jnp.zeros_like(facts)
    facts[0:1, :] = jnp.concatenate([segment, segment], axis=1)
    facts[1:2, :] = jnp.concatenate([weight, weight], axis=1)

    unit = 4

    def match_unit(part, carry):
        first = part * unit
        usable = (mask[pl.ds(first, unit)] & 7) == 0
        masked = jnp.where(usable, pixels[pl.ds(first, unit)].astype(jnp.float32), 0.0)
        masked = masked.astype(jnp.bfloat16).reshape(unit * side_len, side_len)
        columns = jnp.dot(masked, right_ref[...], preferred_element_type=jnp.float32)
        columns = columns.astype(jnp.bfloat16)
        for n in range(unit):
            kernel_set = index_ref[first + n]
            left_parts = []
            for m in range(3):
                even, odd = bands_ref[2 * m], bands_ref[2 * m + 1]
                coef = [table_ref[3 * m + t, kernel_set] for t in range(3)]
                left_parts.append((coef[0] * even + coef[1] * odd).astype(jnp.bfloat16))
                left_parts.append((coef[2] * even).astype(jnp.bfloat16))
            left = jnp.concatenate(left_parts, axis=1)
            own = columns[n * side_len : (n + 1) * side_len]
            stacked = jnp.concatenate(
                [own[:, p * side_len : (p + 1) * side_len] for p in range(6)], axis=0
            )
            start = pl.multiple_of((first + n) * side_len, side_len)
            wide[pl.ds(start, side_len), :] = jnp.dot(left, stacked, preferred_element_type=jnp.float32)
        return carry

    for part in range(LOADS):
        for copy in load_copies(part):
            copy.wait()
        lax.fori_loop(part * load // unit, (part + 1) * load // unit, match_unit, 0)

    pl.semaphore_wait(barrier, jnp.where(adds, GROUP, ADDERS))
    adders(lambda target: facts_copy(target, me).start())

    def send_step(step, carry):
        def gather_rows(target, carry):
            for k in range(PAIR):
                start = target * ROWS + step * PAIR + k
                values = wide[pl.ds(start, blocks, stride=side_len), :].astype(jnp.bfloat16)
                rows[step, target, :, k * side_len : (k + 1) * side_len] = values
            return carry

        lax.fori_loop(0, ADDERS, gather_rows, 0)
        adders(lambda target: rows_copy(step, target, me).start())
        return carry

    lax.fori_loop(0, STEPS, send_step, 0)

    @pl.when(adds)
    def _():
        def keep_own(step, carry):
            held[step, pl.ds(me, 1)] = rows[step, pl.ds(adder, 1)]
            return carry

        lax.fori_loop(0, STEPS, keep_own, 0)
        facts_in[pl.ds(me, 1)] = facts[...].reshape((1,) + facts.shape)
        peers(lambda peer: facts_copy(adder, peer).wait_recv())

        def make_pickers(pair, carry):
            first_lanes = lax.broadcasted_iota(jnp.int32, (1, lanes), 1) < blocks
            segment = jnp.where(first_lanes, facts_in[2 * pair, 0:1, :], facts_in[2 * pair + 1, 0:1, :])
            weight = jnp.where(first_lanes, facts_in[2 * pair, 1:2, :], facts_in[2 * pair + 1, 1:2, :])
            start = pl.multiple_of(pair * lanes, lanes)
            cell = lax.broadcasted_iota(jnp.int32, (cells, lanes), 0).astype(jnp.float32)
            weights[:, pl.ds(start, lanes)] = jnp.where(cell == segment, weight, 0.0).astype(jnp.bfloat16)
            weight_rows[:, pl.ds(start, lanes)] = jnp.broadcast_to(weight, (16, lanes)).astype(jnp.bfloat16)
            segment_column = jnp.broadcast_to(segment, (lanes, lanes)).T
            for c in range(cells // lanes):
                cell = lax.broadcasted_iota(jnp.int32, (lanes, lanes), 1) + c * lanes
                chosen = jnp.where(cell.astype(jnp.float32) == segment_column, 1.0, 0.0)
                picks[pl.ds(start, lanes), c * lanes : (c + 1) * lanes] = chosen.astype(jnp.bfloat16)
            return carry

        lax.fori_loop(0, GROUP // 2, make_pickers, 0)
        part_total = jnp.dot(weight_rows[...], picks[...], preferred_element_type=jnp.float32)
        total_out[...] = part_total[0:8]
        total_copy().start()

    def add_up(step):
        peers(lambda peer: rows_copy(step, adder, peer).wait_recv())
        flat = held[step].reshape(total, width)
        part_sum = jnp.dot(weights[...], flat, preferred_element_type=jnp.float32)
        sums[step] = part_sum
        sums_out[step] = part_sum.astype(jnp.bfloat16)
        sums_copy(step).start()

    def get_scale():
        total_copy().wait_recv()
        scale_row = 1.0 / jnp.maximum(total_out[0:1] + total_in[0:1], 1.0)
        for c in range(cells // lanes):
            scale[c * lanes : (c + 1) * lanes] = jnp.broadcast_to(
                scale_row[:, c * lanes : (c + 1) * lanes], (lanes, lanes)
            ).T

    def take_off(step):
        sums_copy(step).wait_recv()
        whole_sum = sums[step] + sums_in[step].astype(jnp.float32)
        for k in range(PAIR):
            lane = slice(k * side_len, (k + 1) * side_len)
            templates[step, :, lane] = (whole_sum[:, lane] * scale[...]).astype(jnp.bfloat16)
        flat = held[step].reshape(total, width)
        chosen = jnp.dot(picks[...], templates[step], preferred_element_type=jnp.float32)
        change = (flat.astype(jnp.float32) - chosen).astype(jnp.bfloat16)
        diffs[step] = change.reshape(GROUP, blocks, width)
        peers(lambda peer: diffs_copy(step, peer, adder).start())
        places(lambda peer: coadd_copy(step, peer, core).start())
        start = pl.multiple_of(patch * CELLS, CELLS)
        coadd_in[step, pl.ds(core, 1)] = templates[step, pl.ds(start, CELLS)].reshape(1, CELLS, width)
        diffs_in[step, pl.ds(adder, 1)] = diffs[step, pl.ds(me, 1)]

    rows_here = CORES * ROWS

    def wait_coadd(step, source):
        coadd_copy(step, place, source).wait_recv()

    def finish(step):
        adders(lambda source: diffs_copy(step, me, source).wait_recv())

        def spread(source, carry):
            values = diffs_in[step, source].astype(jnp.float32)
            for k in range(PAIR):
                row = source * ROWS + step * PAIR + k
                wide[pl.ds(row, blocks, stride=side_len), :] = values[
                    :, k * side_len : (k + 1) * side_len
                ]
            return carry

        lax.fori_loop(0, ADDERS, spread, 0)
        wait_coadd(step, 1 - core)
        pl.when(jnp.logical_not(adds))(lambda: wait_coadd(step, core))
        for source in range(CORES):
            values = coadd_in[step, source].astype(jnp.float32)
            for k in range(PAIR):
                row = source * ROWS + step * PAIR + k
                coadd_ref[pl.ds(row, CELLS, stride=rows_here), :] = values[
                    :, k * side_len : (k + 1) * side_len
                ]

    lag = 2

    def one_step(step, carry):
        pl.when(adds & (step < STEPS))(lambda: add_up(step))
        pl.when(adds & (step == 1))(get_scale)
        pl.when(adds & (step >= 1) & (step <= STEPS))(lambda: take_off(step - 1))
        pl.when(step >= lag)(lambda: finish(step - lag))
        return carry

    lax.fori_loop(0, STEPS + lag, one_step, 0)

    def narrow(part, carry):
        start = pl.multiple_of(part * 512, 512)
        difference_ref[pl.ds(start, 512), :] = wide[pl.ds(start, 512), :].astype(jnp.bfloat16)
        return carry

    lax.fori_loop(0, wide.shape[0] // 512, narrow, 0)

    adders(lambda target: facts_copy(target, me).wait_send())

    def sent_rows(step, carry):
        adders(lambda target: rows_copy(step, target, me).wait_send())
        return carry

    lax.fori_loop(0, STEPS, sent_rows, 0)

    @pl.when(adds)
    def _():
        total_copy().wait_send()

        def sent(step, carry):
            sums_copy(step).wait_send()
            peers(lambda peer: diffs_copy(step, peer, adder).wait_send())
            places(lambda peer: coadd_copy(step, peer, core).wait_send())
            return carry

        lax.fori_loop(0, STEPS, sent, 0)


def row_shards(pixels, mask_bits, inv_var, owner, cell, coef_index, coef_table):
    blocks, side_len = pixels.shape[0], pixels.shape[1]
    cells = lax.axis_size("patch") * CELLS
    total = GROUP * blocks
    width = PAIR * side_len
    bands = fixed_bands(side_len)
    right_bands = np.transpose(bands, (2, 0, 1)).reshape(side_len, 6 * side_len)
    bf16, f32 = jnp.bfloat16, jnp.float32
    dma = pltpu.SemaphoreType.DMA
    smem, vmem = pl.BlockSpec(memory_space=pltpu.SMEM), pl.BlockSpec(memory_space=pltpu.VMEM)
    coadd, difference = pl.pallas_call(
        trade_kernel,
        in_specs=[smem] * 2 + [vmem] * 5 + [pl.BlockSpec(memory_space=pl.ANY)] * 2,
        out_specs=[vmem] * 2,
        out_shape=[
            jax.ShapeDtypeStruct((CELLS * CORES * ROWS, side_len), f32),
            jax.ShapeDtypeStruct((blocks * side_len, side_len), bf16),
        ],
        scratch_shapes=[
            pltpu.VMEM((blocks, side_len, side_len), bf16),
            pltpu.VMEM((blocks, side_len, side_len), jnp.int32),
            pltpu.VMEM((STEPS, ADDERS, blocks, width), bf16),
            pltpu.VMEM((STEPS, GROUP, blocks, width), bf16),
            pltpu.VMEM((STEPS, cells, width), f32),
            pltpu.VMEM((STEPS, cells, width), bf16),
            pltpu.VMEM((STEPS, cells, width), bf16),
            pltpu.VMEM((STEPS, cells, width), bf16),
            pltpu.VMEM((STEPS, CORES, CELLS, width), bf16),
            pltpu.VMEM((STEPS, GROUP, blocks, width), bf16),
            pltpu.VMEM((STEPS, ADDERS, blocks, width), bf16),
            pltpu.VMEM((cells, total), bf16),
            pltpu.VMEM((total, cells), bf16),
            pltpu.VMEM((blocks * side_len, side_len), f32),
            pltpu.VMEM((8, 2 * blocks), f32),
            pltpu.VMEM((GROUP, 8, 2 * blocks), f32),
            pltpu.VMEM((16, total), bf16),
            pltpu.VMEM((8, cells), f32),
            pltpu.VMEM((8, cells), f32),
            pltpu.VMEM((cells, side_len), f32),
            dma((LOADS,)),
            dma((LOADS,)),
            dma((STEPS, ADDERS)),
            dma((STEPS, GROUP)),
            dma((ADDERS,)),
            dma((GROUP,)),
            dma,
            dma,
            dma((STEPS,)),
            dma((STEPS,)),
            dma((STEPS, HALF)),
            dma((STEPS, CORES)),
            dma((STEPS, GROUP)),
            dma((STEPS, ADDERS)),
        ],
        compiler_params=pltpu.CompilerParams(
            collective_id=0, has_side_effects=True, vmem_limit_bytes=58 * 2**20
        ),
    )(
        coef_index, coef_table.T,
        inv_var.reshape(1, blocks), owner.reshape(1, blocks), cell.reshape(1, blocks),
        jnp.asarray(right_bands, dtype=bf16), jnp.asarray(bands), pixels, mask_bits,
    )
    return (
        coadd.reshape(CELLS, CORES * ROWS, side_len),
        difference.reshape(blocks, side_len, side_len),
    )


def solution(mesh):
    placed = (
        P(("visit", "patch"), None, None),
        P(("visit", "patch"), None, None),
        P(("visit", "patch")),
        P(("visit", "patch")),
        P(("visit", "patch")),
        P(("visit", "patch")),
        P(),
    )
    fits = mesh.shape["visit"] * HALF == GROUP and mesh.shape["patch"] == 2 * HALF
    return jax.shard_map(
        row_shards if fits else shards,
        mesh=mesh,
        in_specs=placed,
        out_specs=(P("patch", "visit", None), P(("visit", "patch"), None, None)),
        check_vma=False,
    )
```

```python
import jax
import jax.numpy as jnp
import numpy as np
from jax import lax
from jax.experimental import pallas as pl
from jax.experimental.pallas import tpu as pltpu
from jax.sharding import PartitionSpec as P

CELLS = 64
KSIZE = 21


gauss_widths = (1.0, 2.0, 3.5)


def band_tables(side_len):
    tap_reach = KSIZE // 2
    position = jnp.arange(side_len).astype(jnp.float32)
    offset = position[:, None] - position[None, :]
    inside = jnp.abs(offset) <= tap_reach
    tap_offsets = jnp.arange(-tap_reach, tap_reach + 1).astype(jnp.float32)
    tables = []
    for spread in gauss_widths:
        profile_sum = jnp.sum(jnp.exp(-tap_offsets * tap_offsets / (2.0 * spread * spread)))
        even_band = jnp.where(
            inside, jnp.exp(-offset * offset / (2.0 * spread * spread)) / profile_sum, 0.0
        )
        tables.append(even_band)
        tables.append(even_band * offset / spread)
    return jnp.stack(tables)


def match_group(blocks, coefficients, tables, right_bands):
    number = blocks.shape[0]
    side_len = blocks.shape[1]
    columns = jnp.dot(
        blocks.reshape(number * side_len, side_len), right_bands, preferred_element_type=jnp.float32
    )
    columns = columns.astype(jnp.bfloat16).reshape(number, side_len, 6, side_len)
    left_parts = []
    for sigma_pos in range(3):
        even_band = tables[2 * sigma_pos]
        odd_band = tables[2 * sigma_pos + 1]
        left_parts.append(
            coefficients[:, 3 * sigma_pos, None, None] * even_band
            + coefficients[:, 3 * sigma_pos + 1, None, None] * odd_band
        )
        left_parts.append(coefficients[:, 3 * sigma_pos + 2, None, None] * even_band)
    left_bands = jnp.stack(left_parts, axis=2).astype(jnp.bfloat16)
    result = jnp.einsum("nisp,npsj->nij", left_bands, columns, preferred_element_type=jnp.float32)
    return result.astype(jnp.bfloat16)


def match_blocks(blocks, coefficients, tables, right_bands):
    number = blocks.shape[0]
    side_len = blocks.shape[1]
    batch_blocks = 16
    rounds = -(-number // batch_blocks)

    def one_batch(bundle):
        return match_group(bundle[0], bundle[1], tables, right_bands)

    matched = lax.map(
        one_batch,
        (
            blocks.reshape(rounds, batch_blocks, side_len, side_len),
            coefficients.reshape(rounds, batch_blocks, coefficients.shape[1]),
        ),
    )
    return matched.reshape(rounds * batch_blocks, side_len, side_len)[:number]


def shards(pixels, mask_bits, inv_var, owner, cell, coef_index, coef_table):
    blocks_here = pixels.shape[0]
    side_len = pixels.shape[1]
    kernel_sets = coef_table.shape[0]
    patches = lax.axis_size("patch")
    visits = lax.axis_size("visit")
    capacity = 4 * blocks_here // patches
    slot_total = patches * capacity
    tables = band_tables(side_len)
    right_bands = (
        jnp.transpose(tables, (2, 0, 1)).reshape(side_len, 6 * side_len).astype(jnp.bfloat16)
    )
    usable = (mask_bits % 2 == 0) & (mask_bits // 2 % 2 == 0) & (mask_bits // 4 % 2 == 0)
    masked = jnp.where(usable, pixels, jnp.zeros((), jnp.bfloat16))
    weight = inv_var.astype(jnp.bfloat16)
    cell_weight = jnp.where(
        cell[:, None] == jnp.arange(CELLS)[None, :], weight[:, None], jnp.zeros((), jnp.bfloat16)
    )
    chosen = (coef_index[:, None] == jnp.arange(kernel_sets)[None, :]).astype(jnp.bfloat16)
    dest_onehot = (owner[:, None] == jnp.arange(patches)[None, :]).astype(jnp.int32)
    slot_rank = jnp.sum((jnp.cumsum(dest_onehot, axis=0) - dest_onehot) * dest_onehot, axis=1)
    slot_of_block = owner * capacity + slot_rank
    matches = slot_of_block[None, :] == jnp.arange(slot_total)[:, None]
    source_row = jnp.sum(jnp.where(matches, jnp.arange(blocks_here)[None, :], 0), axis=1)
    filled = jnp.any(matches, axis=1)

    def pack_slots(values):
        picked = values[source_row]
        keep_rows = filled.reshape((slot_total,) + (1,) * (values.ndim - 1))
        picked = jnp.where(keep_rows, picked, jnp.zeros((), values.dtype))
        return picked.reshape((patches, capacity) + values.shape[1:])

    pieces = lax.all_to_all(pack_slots(masked), "patch", split_axis=0, concat_axis=0, tiled=True)
    weights = lax.all_to_all(
        pack_slots(cell_weight), "patch", split_axis=0, concat_axis=0, tiled=True
    )
    kernel_picks = lax.all_to_all(
        pack_slots(chosen), "patch", split_axis=0, concat_axis=0, tiled=True
    )
    flat_blocks = pieces.reshape((-1, side_len, side_len))
    coefficients = jnp.dot(
        kernel_picks.reshape(-1, kernel_sets).astype(jnp.float32),
        coef_table,
        precision=lax.Precision.HIGHEST,
    )
    matched = match_blocks(flat_blocks, coefficients, tables, right_bands)
    matched_slots = matched.reshape(pieces.shape)
    flat_weights = weights.reshape(slot_total, CELLS)
    flat_matched = matched_slots.reshape(slot_total, side_len * side_len)
    numerator = jnp.einsum(
        "sc,sk->ck", flat_weights, flat_matched, preferred_element_type=jnp.float32
    ).reshape(CELLS, side_len, side_len)
    weight_sum = jnp.sum(flat_weights.astype(jnp.float32), axis=0)
    rows_here = side_len // visits
    numerator, weight_sum = lax.psum((numerator, weight_sum), "visit")
    coadd_full = numerator / jnp.maximum(weight_sum, 1.0)[:, None, None]
    coadd_part = lax.dynamic_slice_in_dim(
        coadd_full, lax.axis_index("visit") * rows_here, rows_here, 1
    )
    template = coadd_full.astype(jnp.bfloat16)
    live_slots = (flat_weights > 0).astype(jnp.bfloat16)
    slot_template = jnp.einsum(
        "sc,ck->sk",
        live_slots,
        template.reshape(CELLS, side_len * side_len),
        preferred_element_type=jnp.float32,
    )
    difference_slots = (flat_matched.astype(jnp.float32) - slot_template).astype(jnp.bfloat16)
    returned = lax.all_to_all(
        difference_slots.reshape(patches, capacity, side_len, side_len),
        "patch",
        split_axis=0,
        concat_axis=0,
        tiled=True,
    )
    difference = returned.reshape(slot_total, side_len, side_len)[slot_of_block]
    return (coadd_part, difference)


PLANE = 8
CORES = 2
ROWS = 16
STEPS = 8
PAIR = ROWS // STEPS
LOADS = 4
MESH = pl.DeviceIdType.MESH


def fixed_bands(side_len):
    reach = KSIZE // 2
    position = np.arange(side_len, dtype=np.float32)
    offset = position[:, None] - position[None, :]
    taps = np.arange(-reach, reach + 1).astype(np.float32)
    tables = []
    for spread in gauss_widths:
        spread = np.float32(spread)
        total = np.sum(np.exp(-taps * taps / (2 * spread * spread)))
        even = np.where(np.abs(offset) <= reach, np.exp(-offset * offset / (2 * spread * spread)) / total, 0)
        tables.append(even.astype(np.float32))
        tables.append((even * offset / spread).astype(np.float32))
    return np.stack(tables)


def trade_kernel(
    index_ref, table_ref, inv_var_ref, owner_ref, cell_ref, right_ref, bands_ref, pixels_hbm, mask_hbm,
    coadd_ref, difference_ref,
    pixels, mask, rows, held, sums, sums_out, near_in, cross_in, templates, coadd_in, diffs, diffs_in,
    weights, picks, wide, facts, facts_in, weight_rows, total_out, total_near, total_in, scale,
    load_pixels, load_mask, send_rows, recv_rows, send_facts, recv_facts,
    send_total, recv_total_near, recv_total_cross, send_near, recv_near, send_cross, recv_cross,
    send_back, recv_back, send_coadd, recv_coadd, send_diffs, recv_diffs,
):
    blocks, side_len = pixels.shape[0], pixels.shape[1]
    total = PLANE * blocks
    cells = weights.shape[0]
    width = PAIR * side_len
    lanes = 2 * blocks
    load = blocks // LOADS
    visit, patch = lax.axis_index("visit"), lax.axis_index("patch")
    layer, core = patch // CORES, patch % CORES
    me = visit * CORES + core
    inner = (layer + 1) // 2 == 1
    outer = jnp.logical_not(inner)
    mate = (visit, (layer + 1 - 2 * (layer % 2)) * CORES + core)
    across = (visit, (3 - layer) * CORES + core)
    barrier = pltpu.get_barrier_semaphore()

    def device_of(index):
        return (index // CORES, layer * CORES + index % CORES)

    def peers(act):
        def one(turn, carry):
            act((me + turn) % PLANE)
            return carry

        lax.fori_loop(1, PLANE, one, 0)

    def greet(device):
        pl.semaphore_signal(barrier, inc=1, device_id=device, device_id_type=MESH)

    def load_copies(part):
        span = pl.ds(part * load, load)
        return (
            pltpu.make_async_copy(pixels_hbm.at[span], pixels.at[span], load_pixels.at[part]),
            pltpu.make_async_copy(mask_hbm.at[span], mask.at[span], load_mask.at[part]),
        )

    def send(source, target, send_sem, recv_sem, device):
        return pltpu.make_async_remote_copy(
            src_ref=source, dst_ref=target, send_sem=send_sem, recv_sem=recv_sem,
            device_id=device, device_id_type=MESH,
        )

    def facts_copy(peer, slot):
        return send(facts, facts_in.at[slot], send_facts.at[peer], recv_facts.at[slot], device_of(peer))

    def rows_copy(step, peer, slot):
        return send(
            rows.at[step, peer], held.at[step, slot],
            send_rows.at[step, peer], recv_rows.at[step, slot], device_of(peer),
        )

    def total_near_copy():
        return send(total_out, total_near, send_total, recv_total_near, mate)

    def total_cross_copy():
        return send(total_out, total_in, send_total, recv_total_cross, across)

    def near_copy(step):
        return send(sums_out.at[step], near_in.at[step], send_near.at[step], recv_near.at[step], mate)

    def cross_copy(step):
        return send(sums_out.at[step], cross_in.at[step], send_cross.at[step], recv_cross.at[step], across)

    def back_copy(step):
        return send(templates.at[step], templates.at[step], send_back.at[step], recv_back.at[step], mate)

    def coadd_copy(step):
        start = pl.multiple_of((layer * CORES + 1 - core) * CELLS, CELLS)
        return send(
            templates.at[step, pl.ds(start, CELLS)], coadd_in.at[step],
            send_coadd.at[step], recv_coadd.at[step], (visit, layer * CORES + 1 - core),
        )

    def diffs_copy(step, peer, slot):
        return send(
            diffs.at[step, peer], diffs_in.at[step, slot],
            send_diffs.at[step, peer], recv_diffs.at[step, slot], device_of(peer),
        )

    for part in range(LOADS):
        for copy in load_copies(part):
            copy.start()

    peers(lambda peer: greet(device_of(peer)))
    greet(mate)
    pl.when(inner)(lambda: greet(across))

    segment = (owner_ref[...] * CELLS + cell_ref[...]).astype(jnp.float32)
    weight = inv_var_ref[...].astype(jnp.bfloat16).astype(jnp.float32)
    facts[...] = jnp.zeros_like(facts)
    facts[0:1, :] = jnp.concatenate([segment, segment], axis=1)
    facts[1:2, :] = jnp.concatenate([weight, weight], axis=1)

    unit = 4

    def match_unit(part, carry):
        first = part * unit
        usable = (mask[pl.ds(first, unit)] & 7) == 0
        masked = jnp.where(usable, pixels[pl.ds(first, unit)].astype(jnp.float32), 0.0)
        masked = masked.astype(jnp.bfloat16).reshape(unit * side_len, side_len)
        columns = jnp.dot(masked, right_ref[...], preferred_element_type=jnp.float32)
        columns = columns.astype(jnp.bfloat16)
        for n in range(unit):
            kernel_set = index_ref[first + n]
            left_parts = []
            for m in range(3):
                even, odd = bands_ref[2 * m], bands_ref[2 * m + 1]
                coef = [table_ref[3 * m + t, kernel_set] for t in range(3)]
                left_parts.append((coef[0] * even + coef[1] * odd).astype(jnp.bfloat16))
                left_parts.append((coef[2] * even).astype(jnp.bfloat16))
            left = jnp.concatenate(left_parts, axis=1)
            own = columns[n * side_len : (n + 1) * side_len]
            stacked = jnp.concatenate(
                [own[:, p * side_len : (p + 1) * side_len] for p in range(6)], axis=0
            )
            start = pl.multiple_of((first + n) * side_len, side_len)
            wide[pl.ds(start, side_len), :] = jnp.dot(left, stacked, preferred_element_type=jnp.float32)
        return carry

    for part in range(LOADS):
        for copy in load_copies(part):
            copy.wait()
        lax.fori_loop(part * load // unit, (part + 1) * load // unit, match_unit, 0)

    pl.semaphore_wait(barrier, jnp.where(inner, PLANE + 1, PLANE))
    peers(lambda peer: facts_copy(peer, me).start())

    def send_rows_of(step):
        def gather_rows(peer, carry):
            for k in range(PAIR):
                start = peer * ROWS + step * PAIR + k
                values = wide[pl.ds(start, blocks, stride=side_len), :].astype(jnp.bfloat16)
                rows[step, peer, :, k * side_len : (k + 1) * side_len] = values
            return carry

        lax.fori_loop(0, PLANE, gather_rows, 0)
        peers(lambda peer: rows_copy(step, peer, me).start())
        held[step, pl.ds(me, 1)] = rows[step, pl.ds(me, 1)]

    ahead = 2
    for step in range(ahead):
        send_rows_of(step)
    facts_in[pl.ds(me, 1)] = facts[...].reshape((1,) + facts.shape)
    peers(lambda peer: facts_copy(peer, peer).wait_recv())

    def make_pickers(pair, carry):
        first_lanes = lax.broadcasted_iota(jnp.int32, (1, lanes), 1) < blocks
        segment = jnp.where(first_lanes, facts_in[2 * pair, 0:1, :], facts_in[2 * pair + 1, 0:1, :])
        weight = jnp.where(first_lanes, facts_in[2 * pair, 1:2, :], facts_in[2 * pair + 1, 1:2, :])
        start = pl.multiple_of(pair * lanes, lanes)
        cell = lax.broadcasted_iota(jnp.int32, (cells, lanes), 0).astype(jnp.float32)
        weights[:, pl.ds(start, lanes)] = jnp.where(cell == segment, weight, 0.0).astype(jnp.bfloat16)
        weight_rows[:, pl.ds(start, lanes)] = jnp.broadcast_to(weight, (16, lanes)).astype(jnp.bfloat16)
        segment_column = jnp.broadcast_to(segment, (lanes, lanes)).T
        for c in range(cells // lanes):
            cell = lax.broadcasted_iota(jnp.int32, (lanes, lanes), 1) + c * lanes
            chosen = jnp.where(cell.astype(jnp.float32) == segment_column, 1.0, 0.0)
            picks[pl.ds(start, lanes), c * lanes : (c + 1) * lanes] = chosen.astype(jnp.bfloat16)
        return carry

    lax.fori_loop(0, PLANE // 2, make_pickers, 0)
    part_total = jnp.dot(weight_rows[...], picks[...], preferred_element_type=jnp.float32)
    total_out[...] = part_total[0:8]
    pl.when(outer)(lambda: total_near_copy().start())

    def add_up(step):
        peers(lambda peer: rows_copy(step, peer, peer).wait_recv())
        flat = held[step].reshape(total, width)
        part_sum = jnp.dot(weights[...], flat, preferred_element_type=jnp.float32)

        @pl.when(inner)
        def _():
            sums[step] = part_sum

        @pl.when(outer)
        def _():
            sums_out[step] = part_sum.astype(jnp.bfloat16)
            near_copy(step).start()

    def join_totals():
        total_near_copy().wait_recv()
        total_out[...] += total_near[...]
        total_cross_copy().start()

    def join(step):
        near_copy(step).wait_recv()
        joint = sums[step] + near_in[step].astype(jnp.float32)
        sums[step] = joint
        sums_out[step] = joint.astype(jnp.bfloat16)
        cross_copy(step).start()

    def get_scale():
        total_cross_copy().wait_recv()
        scale_row = 1.0 / jnp.maximum(total_out[0:1] + total_in[0:1], 1.0)
        for c in range(cells // lanes):
            scale[c * lanes : (c + 1) * lanes] = jnp.broadcast_to(
                scale_row[:, c * lanes : (c + 1) * lanes], (lanes, lanes)
            ).T

    def settle(step):
        cross_copy(step).wait_recv()
        whole_sum = sums[step] + cross_in[step].astype(jnp.float32)
        for k in range(PAIR):
            lane = slice(k * side_len, (k + 1) * side_len)
            templates[step, :, lane] = (whole_sum[:, lane] * scale[...]).astype(jnp.bfloat16)
        back_copy(step).start()

    def take_off(step):
        flat = held[step].reshape(total, width)
        chosen = jnp.dot(picks[...], templates[step], preferred_element_type=jnp.float32)
        change = (flat.astype(jnp.float32) - chosen).astype(jnp.bfloat16)
        diffs[step] = change.reshape(PLANE, blocks, width)
        peers(lambda peer: diffs_copy(step, peer, me).start())
        coadd_copy(step).start()
        diffs_in[step, pl.ds(me, 1)] = diffs[step, pl.ds(me, 1)]

    rows_here = CORES * ROWS

    def finish(step):
        start = pl.multiple_of(patch * CELLS, CELLS)
        own = templates[step, pl.ds(start, CELLS)].astype(jnp.float32)
        for k in range(PAIR):
            row = core * ROWS + step * PAIR + k
            coadd_ref[pl.ds(row, CELLS, stride=rows_here), :] = own[:, k * side_len : (k + 1) * side_len]
        peers(lambda peer: diffs_copy(step, peer, peer).wait_recv())

        def spread(source, carry):
            values = diffs_in[step, source].astype(jnp.float32)
            for k in range(PAIR):
                row = source * ROWS + step * PAIR + k
                wide[pl.ds(row, blocks, stride=side_len), :] = values[
                    :, k * side_len : (k + 1) * side_len
                ]
            return carry

        lax.fori_loop(0, PLANE, spread, 0)
        coadd_copy(step).wait_recv()
        other = coadd_in[step].astype(jnp.float32)
        for k in range(PAIR):
            row = (1 - core) * ROWS + step * PAIR + k
            coadd_ref[pl.ds(row, CELLS, stride=rows_here), :] = other[:, k * side_len : (k + 1) * side_len]

    def one_step(step, carry):
        pl.when(step < STEPS)(lambda: add_up(step))
        pl.when(step + ahead < STEPS)(lambda: send_rows_of(step + ahead))

        @pl.when(inner)
        def _():
            pl.when(step == 1)(join_totals)
            pl.when((step >= 1) & (step <= STEPS))(lambda: join(step - 1))
            pl.when(step == 2)(get_scale)
            pl.when((step >= 2) & (step <= STEPS + 1))(lambda: settle(step - 2))

        late = jnp.where(inner, 2, 3)

        @pl.when((step >= late) & (step < STEPS + late))
        def _():
            pl.when(outer)(lambda: back_copy(step - late).wait_recv())
            take_off(step - late)

        pl.when(step >= 4)(lambda: finish(step - 4))
        return carry

    lax.fori_loop(0, STEPS + 4, one_step, 0)

    def narrow(part, carry):
        start = pl.multiple_of(part * 512, 512)
        difference_ref[pl.ds(start, 512), :] = wide[pl.ds(start, 512), :].astype(jnp.bfloat16)
        return carry

    lax.fori_loop(0, wide.shape[0] // 512, narrow, 0)

    peers(lambda peer: facts_copy(peer, me).wait_send())
    pl.when(inner)(lambda: total_cross_copy().wait_send())
    pl.when(outer)(lambda: total_near_copy().wait_send())

    def sent(step, carry):
        peers(lambda peer: rows_copy(step, peer, me).wait_send())
        peers(lambda peer: diffs_copy(step, peer, me).wait_send())
        coadd_copy(step).wait_send()

        @pl.when(inner)
        def _():
            cross_copy(step).wait_send()
            back_copy(step).wait_send()

        pl.when(outer)(lambda: near_copy(step).wait_send())
        return carry

    lax.fori_loop(0, STEPS, sent, 0)


def row_shards(pixels, mask_bits, inv_var, owner, cell, coef_index, coef_table):
    blocks, side_len = pixels.shape[0], pixels.shape[1]
    cells = lax.axis_size("patch") * CELLS
    total = PLANE * blocks
    width = PAIR * side_len
    bands = fixed_bands(side_len)
    right_bands = np.transpose(bands, (2, 0, 1)).reshape(side_len, 6 * side_len)
    bf16, f32 = jnp.bfloat16, jnp.float32
    dma = pltpu.SemaphoreType.DMA
    smem, vmem = pl.BlockSpec(memory_space=pltpu.SMEM), pl.BlockSpec(memory_space=pltpu.VMEM)
    coadd, difference = pl.pallas_call(
        trade_kernel,
        in_specs=[smem] * 2 + [vmem] * 5 + [pl.BlockSpec(memory_space=pl.ANY)] * 2,
        out_specs=[vmem] * 2,
        out_shape=[
            jax.ShapeDtypeStruct((CELLS * CORES * ROWS, side_len), f32),
            jax.ShapeDtypeStruct((blocks * side_len, side_len), bf16),
        ],
        scratch_shapes=[
            pltpu.VMEM((blocks, side_len, side_len), bf16),
            pltpu.VMEM((blocks, side_len, side_len), jnp.int32),
            pltpu.VMEM((STEPS, PLANE, blocks, width), bf16),
            pltpu.VMEM((STEPS, PLANE, blocks, width), bf16),
            pltpu.VMEM((STEPS, cells, width), f32),
            pltpu.VMEM((STEPS, cells, width), bf16),
            pltpu.VMEM((STEPS, cells, width), bf16),
            pltpu.VMEM((STEPS, cells, width), bf16),
            pltpu.VMEM((STEPS, cells, width), bf16),
            pltpu.VMEM((STEPS, CELLS, width), bf16),
            pltpu.VMEM((STEPS, PLANE, blocks, width), bf16),
            pltpu.VMEM((STEPS, PLANE, blocks, width), bf16),
            pltpu.VMEM((cells, total), bf16),
            pltpu.VMEM((total, cells), bf16),
            pltpu.VMEM((blocks * side_len, side_len), f32),
            pltpu.VMEM((8, 2 * blocks), f32),
            pltpu.VMEM((PLANE, 8, 2 * blocks), f32),
            pltpu.VMEM((16, total), bf16),
            pltpu.VMEM((8, cells), f32),
            pltpu.VMEM((8, cells), f32),
            pltpu.VMEM((8, cells), f32),
            pltpu.VMEM((cells, side_len), f32),
            dma((LOADS,)),
            dma((LOADS,)),
            dma((STEPS, PLANE)),
            dma((STEPS, PLANE)),
            dma((PLANE,)),
            dma((PLANE,)),
            dma,
            dma,
            dma,
        ]
        + [dma((STEPS,))] * 8
        + [dma((STEPS, PLANE))] * 2,
        compiler_params=pltpu.CompilerParams(
            collective_id=0, has_side_effects=True, vmem_limit_bytes=58 * 2**20
        ),
    )(
        coef_index, coef_table.T,
        inv_var.reshape(1, blocks), owner.reshape(1, blocks), cell.reshape(1, blocks),
        jnp.asarray(right_bands, dtype=bf16), jnp.asarray(bands), pixels, mask_bits,
    )
    return (
        coadd.reshape(CELLS, CORES * ROWS, side_len),
        difference.reshape(blocks, side_len, side_len),
    )


def solution(mesh):
    placed = (
        P(("visit", "patch"), None, None),
        P(("visit", "patch"), None, None),
        P(("visit", "patch")),
        P(("visit", "patch")),
        P(("visit", "patch")),
        P(("visit", "patch")),
        P(),
    )
    fits = mesh.shape["visit"] * CORES == PLANE and mesh.shape["patch"] == 4 * CORES
    return jax.shard_map(
        row_shards if fits else shards,
        mesh=mesh,
        in_specs=placed,
        out_specs=(P("patch", "visit", None), P(("visit", "patch"), None, None)),
        check_vma=False,
    )
```

```python
import jax
import jax.numpy as jnp
import numpy as np
from jax import lax
from jax.experimental import pallas as pl
from jax.experimental.pallas import tpu as pltpu
from jax.sharding import PartitionSpec as P

CELLS = 64
KSIZE = 21


gauss_widths = (1.0, 2.0, 3.5)


def band_tables(side_len):
    tap_reach = KSIZE // 2
    position = jnp.arange(side_len).astype(jnp.float32)
    offset = position[:, None] - position[None, :]
    inside = jnp.abs(offset) <= tap_reach
    tap_offsets = jnp.arange(-tap_reach, tap_reach + 1).astype(jnp.float32)
    tables = []
    for spread in gauss_widths:
        profile_sum = jnp.sum(jnp.exp(-tap_offsets * tap_offsets / (2.0 * spread * spread)))
        even_band = jnp.where(
            inside, jnp.exp(-offset * offset / (2.0 * spread * spread)) / profile_sum, 0.0
        )
        tables.append(even_band)
        tables.append(even_band * offset / spread)
    return jnp.stack(tables)


def match_group(blocks, coefficients, tables, right_bands):
    number = blocks.shape[0]
    side_len = blocks.shape[1]
    columns = jnp.dot(
        blocks.reshape(number * side_len, side_len), right_bands, preferred_element_type=jnp.float32
    )
    columns = columns.astype(jnp.bfloat16).reshape(number, side_len, 6, side_len)
    left_parts = []
    for sigma_pos in range(3):
        even_band = tables[2 * sigma_pos]
        odd_band = tables[2 * sigma_pos + 1]
        left_parts.append(
            coefficients[:, 3 * sigma_pos, None, None] * even_band
            + coefficients[:, 3 * sigma_pos + 1, None, None] * odd_band
        )
        left_parts.append(coefficients[:, 3 * sigma_pos + 2, None, None] * even_band)
    left_bands = jnp.stack(left_parts, axis=2).astype(jnp.bfloat16)
    result = jnp.einsum("nisp,npsj->nij", left_bands, columns, preferred_element_type=jnp.float32)
    return result.astype(jnp.bfloat16)


def match_blocks(blocks, coefficients, tables, right_bands):
    number = blocks.shape[0]
    side_len = blocks.shape[1]
    batch_blocks = 16
    rounds = -(-number // batch_blocks)

    def one_batch(bundle):
        return match_group(bundle[0], bundle[1], tables, right_bands)

    matched = lax.map(
        one_batch,
        (
            blocks.reshape(rounds, batch_blocks, side_len, side_len),
            coefficients.reshape(rounds, batch_blocks, coefficients.shape[1]),
        ),
    )
    return matched.reshape(rounds * batch_blocks, side_len, side_len)[:number]


def shards(pixels, mask_bits, inv_var, owner, cell, coef_index, coef_table):
    blocks_here = pixels.shape[0]
    side_len = pixels.shape[1]
    kernel_sets = coef_table.shape[0]
    patches = lax.axis_size("patch")
    visits = lax.axis_size("visit")
    capacity = 4 * blocks_here // patches
    slot_total = patches * capacity
    tables = band_tables(side_len)
    right_bands = (
        jnp.transpose(tables, (2, 0, 1)).reshape(side_len, 6 * side_len).astype(jnp.bfloat16)
    )
    usable = (mask_bits % 2 == 0) & (mask_bits // 2 % 2 == 0) & (mask_bits // 4 % 2 == 0)
    masked = jnp.where(usable, pixels, jnp.zeros((), jnp.bfloat16))
    weight = inv_var.astype(jnp.bfloat16)
    cell_weight = jnp.where(
        cell[:, None] == jnp.arange(CELLS)[None, :], weight[:, None], jnp.zeros((), jnp.bfloat16)
    )
    chosen = (coef_index[:, None] == jnp.arange(kernel_sets)[None, :]).astype(jnp.bfloat16)
    dest_onehot = (owner[:, None] == jnp.arange(patches)[None, :]).astype(jnp.int32)
    slot_rank = jnp.sum((jnp.cumsum(dest_onehot, axis=0) - dest_onehot) * dest_onehot, axis=1)
    slot_of_block = owner * capacity + slot_rank
    matches = slot_of_block[None, :] == jnp.arange(slot_total)[:, None]
    source_row = jnp.sum(jnp.where(matches, jnp.arange(blocks_here)[None, :], 0), axis=1)
    filled = jnp.any(matches, axis=1)

    def pack_slots(values):
        picked = values[source_row]
        keep_rows = filled.reshape((slot_total,) + (1,) * (values.ndim - 1))
        picked = jnp.where(keep_rows, picked, jnp.zeros((), values.dtype))
        return picked.reshape((patches, capacity) + values.shape[1:])

    pieces = lax.all_to_all(pack_slots(masked), "patch", split_axis=0, concat_axis=0, tiled=True)
    weights = lax.all_to_all(
        pack_slots(cell_weight), "patch", split_axis=0, concat_axis=0, tiled=True
    )
    kernel_picks = lax.all_to_all(
        pack_slots(chosen), "patch", split_axis=0, concat_axis=0, tiled=True
    )
    flat_blocks = pieces.reshape((-1, side_len, side_len))
    coefficients = jnp.dot(
        kernel_picks.reshape(-1, kernel_sets).astype(jnp.float32),
        coef_table,
        precision=lax.Precision.HIGHEST,
    )
    matched = match_blocks(flat_blocks, coefficients, tables, right_bands)
    matched_slots = matched.reshape(pieces.shape)
    flat_weights = weights.reshape(slot_total, CELLS)
    flat_matched = matched_slots.reshape(slot_total, side_len * side_len)
    numerator = jnp.einsum(
        "sc,sk->ck", flat_weights, flat_matched, preferred_element_type=jnp.float32
    ).reshape(CELLS, side_len, side_len)
    weight_sum = jnp.sum(flat_weights.astype(jnp.float32), axis=0)
    rows_here = side_len // visits
    numerator, weight_sum = lax.psum((numerator, weight_sum), "visit")
    coadd_full = numerator / jnp.maximum(weight_sum, 1.0)[:, None, None]
    coadd_part = lax.dynamic_slice_in_dim(
        coadd_full, lax.axis_index("visit") * rows_here, rows_here, 1
    )
    template = coadd_full.astype(jnp.bfloat16)
    live_slots = (flat_weights > 0).astype(jnp.bfloat16)
    slot_template = jnp.einsum(
        "sc,ck->sk",
        live_slots,
        template.reshape(CELLS, side_len * side_len),
        preferred_element_type=jnp.float32,
    )
    difference_slots = (flat_matched.astype(jnp.float32) - slot_template).astype(jnp.bfloat16)
    returned = lax.all_to_all(
        difference_slots.reshape(patches, capacity, side_len, side_len),
        "patch",
        split_axis=0,
        concat_axis=0,
        tiled=True,
    )
    difference = returned.reshape(slot_total, side_len, side_len)[slot_of_block]
    return (coadd_part, difference)


PLANE = 8
CORES = 2
ROWS = 16
STEPS = 8
PAIR = ROWS // STEPS
LOADS = 4
PARTS = 4
MESH = pl.DeviceIdType.MESH


def fixed_bands(side_len):
    reach = KSIZE // 2
    position = np.arange(side_len, dtype=np.float32)
    offset = position[:, None] - position[None, :]
    taps = np.arange(-reach, reach + 1).astype(np.float32)
    tables = []
    for spread in gauss_widths:
        spread = np.float32(spread)
        total = np.sum(np.exp(-taps * taps / (2 * spread * spread)))
        even = np.where(np.abs(offset) <= reach, np.exp(-offset * offset / (2 * spread * spread)) / total, 0)
        tables.append(even.astype(np.float32))
        tables.append((even * offset / spread).astype(np.float32))
    return np.stack(tables)


def trade_kernel(
    index_ref, table_ref, inv_var_ref, owner_ref, cell_ref, right_ref, bands_ref, pixels_hbm, mask_hbm,
    coadd_ref, difference_ref,
    pixels, mask, rows, held, sums, sums_out, near_in, cross_in, templates, coadd_in, diffs, diffs_in,
    weights, picks, wide, facts, facts_in, weight_rows, total_out, total_near, total_in, scale,
    load_pixels, load_mask, send_rows, recv_rows, send_facts, recv_facts,
    send_total, recv_total_near, recv_total_cross, send_near, recv_near, send_cross, recv_cross,
    send_back, recv_back, send_coadd, recv_coadd, send_diffs, recv_diffs,
):
    blocks, side_len = pixels.shape[0], pixels.shape[1]
    total = PLANE * blocks
    cells = weights.shape[0]
    width = PAIR * side_len
    lanes = 2 * blocks
    load = blocks // LOADS
    visit, patch = lax.axis_index("visit"), lax.axis_index("patch")
    layer, core = patch // CORES, patch % CORES
    me = visit * CORES + core
    inner = (layer + 1) // 2 == 1
    outer = jnp.logical_not(inner)
    mate = (visit, (layer + 1 - 2 * (layer % 2)) * CORES + core)
    across = (visit, (3 - layer) * CORES + core)
    barrier = pltpu.get_barrier_semaphore()

    def device_of(index):
        return (index // CORES, layer * CORES + index % CORES)

    def peers(act):
        def one(turn, carry):
            act((me + turn) % PLANE)
            return carry

        lax.fori_loop(1, PLANE, one, 0)

    def greet(device):
        pl.semaphore_signal(barrier, inc=1, device_id=device, device_id_type=MESH)

    def load_copies(part):
        span = pl.ds(part * load, load)
        return (
            pltpu.make_async_copy(pixels_hbm.at[span], pixels.at[span], load_pixels.at[part]),
            pltpu.make_async_copy(mask_hbm.at[span], mask.at[span], load_mask.at[part]),
        )

    def send(source, target, send_sem, recv_sem, device):
        return pltpu.make_async_remote_copy(
            src_ref=source, dst_ref=target, send_sem=send_sem, recv_sem=recv_sem,
            device_id=device, device_id_type=MESH,
        )

    def facts_copy(peer, slot):
        return send(facts, facts_in.at[slot], send_facts.at[peer], recv_facts.at[slot], device_of(peer))

    def rows_copy(step, peer, slot):
        return send(
            rows.at[step, peer], held.at[step, slot],
            send_rows.at[step, peer], recv_rows.at[step, slot], device_of(peer),
        )

    def total_near_copy():
        return send(total_out, total_near, send_total, recv_total_near, mate)

    def total_cross_copy():
        return send(total_out, total_in, send_total, recv_total_cross, across)

    some = cells // PARTS

    def cells_of(part):
        return pl.ds(pl.multiple_of(part * some, some), some)

    def every_part(act):
        def one(part, carry):
            act(part)
            return carry

        lax.fori_loop(0, PARTS, one, 0)

    def near_copy(step, part):
        span = cells_of(part)
        return send(
            sums_out.at[step, span], near_in.at[step, span],
            send_near.at[step, part], recv_near.at[step, part], mate,
        )

    def cross_copy(step, part):
        span = cells_of(part)
        return send(
            sums_out.at[step, span], cross_in.at[step, span],
            send_cross.at[step, part], recv_cross.at[step, part], across,
        )

    def back_copy(step, part):
        span = cells_of(part)
        return send(
            templates.at[step, span], templates.at[step, span],
            send_back.at[step, part], recv_back.at[step, part], mate,
        )

    def coadd_copy(step):
        start = pl.multiple_of((layer * CORES + 1 - core) * CELLS, CELLS)
        return send(
            templates.at[step, pl.ds(start, CELLS)], coadd_in.at[step],
            send_coadd.at[step], recv_coadd.at[step], (visit, layer * CORES + 1 - core),
        )

    def diffs_copy(step, peer, slot):
        return send(
            diffs.at[step, peer], diffs_in.at[step, slot],
            send_diffs.at[step, peer], recv_diffs.at[step, slot], device_of(peer),
        )

    for part in range(LOADS):
        for copy in load_copies(part):
            copy.start()

    peers(lambda peer: greet(device_of(peer)))
    greet(mate)
    pl.when(inner)(lambda: greet(across))

    segment = (owner_ref[...] * CELLS + cell_ref[...]).astype(jnp.float32)
    weight = inv_var_ref[...].astype(jnp.bfloat16).astype(jnp.float32)
    facts[...] = jnp.zeros_like(facts)
    facts[0:1, :] = jnp.concatenate([segment, segment], axis=1)
    facts[1:2, :] = jnp.concatenate([weight, weight], axis=1)

    unit = 4

    def match_unit(part, carry):
        first = part * unit
        usable = (mask[pl.ds(first, unit)] & 7) == 0
        masked = jnp.where(usable, pixels[pl.ds(first, unit)].astype(jnp.float32), 0.0)
        masked = masked.astype(jnp.bfloat16).reshape(unit * side_len, side_len)
        columns = jnp.dot(masked, right_ref[...], preferred_element_type=jnp.float32)
        columns = columns.astype(jnp.bfloat16)
        for n in range(unit):
            kernel_set = index_ref[first + n]
            left_parts = []
            for m in range(3):
                even, odd = bands_ref[2 * m], bands_ref[2 * m + 1]
                coef = [table_ref[3 * m + t, kernel_set] for t in range(3)]
                left_parts.append((coef[0] * even + coef[1] * odd).astype(jnp.bfloat16))
                left_parts.append((coef[2] * even).astype(jnp.bfloat16))
            left = jnp.concatenate(left_parts, axis=1)
            own = columns[n * side_len : (n + 1) * side_len]
            stacked = jnp.concatenate(
                [own[:, p * side_len : (p + 1) * side_len] for p in range(6)], axis=0
            )
            start = pl.multiple_of((first + n) * side_len, side_len)
            wide[pl.ds(start, side_len), :] = jnp.dot(left, stacked, preferred_element_type=jnp.float32)
        return carry

    for part in range(LOADS):
        for copy in load_copies(part):
            copy.wait()
        lax.fori_loop(part * load // unit, (part + 1) * load // unit, match_unit, 0)

    pl.semaphore_wait(barrier, jnp.where(inner, PLANE + 1, PLANE))
    peers(lambda peer: facts_copy(peer, me).start())

    def send_rows_of(step):
        def gather_rows(peer, carry):
            for k in range(PAIR):
                start = peer * ROWS + step * PAIR + k
                values = wide[pl.ds(start, blocks, stride=side_len), :].astype(jnp.bfloat16)
                rows[step, peer, :, k * side_len : (k + 1) * side_len] = values
            return carry

        lax.fori_loop(0, PLANE, gather_rows, 0)
        peers(lambda peer: rows_copy(step, peer, me).start())
        held[step, pl.ds(me, 1)] = rows[step, pl.ds(me, 1)]

    ahead = 2
    for step in range(ahead):
        send_rows_of(step)
    facts_in[pl.ds(me, 1)] = facts[...].reshape((1,) + facts.shape)
    peers(lambda peer: facts_copy(peer, peer).wait_recv())

    def make_pickers(pair, carry):
        first_lanes = lax.broadcasted_iota(jnp.int32, (1, lanes), 1) < blocks
        segment = jnp.where(first_lanes, facts_in[2 * pair, 0:1, :], facts_in[2 * pair + 1, 0:1, :])
        weight = jnp.where(first_lanes, facts_in[2 * pair, 1:2, :], facts_in[2 * pair + 1, 1:2, :])
        start = pl.multiple_of(pair * lanes, lanes)
        cell = lax.broadcasted_iota(jnp.int32, (cells, lanes), 0).astype(jnp.float32)
        weights[:, pl.ds(start, lanes)] = jnp.where(cell == segment, weight, 0.0).astype(jnp.bfloat16)
        weight_rows[:, pl.ds(start, lanes)] = jnp.broadcast_to(weight, (16, lanes)).astype(jnp.bfloat16)
        segment_column = jnp.broadcast_to(segment, (lanes, lanes)).T
        for c in range(cells // lanes):
            cell = lax.broadcasted_iota(jnp.int32, (lanes, lanes), 1) + c * lanes
            chosen = jnp.where(cell.astype(jnp.float32) == segment_column, 1.0, 0.0)
            picks[pl.ds(start, lanes), c * lanes : (c + 1) * lanes] = chosen.astype(jnp.bfloat16)
        return carry

    lax.fori_loop(0, PLANE // 2, make_pickers, 0)
    part_total = jnp.dot(weight_rows[...], picks[...], preferred_element_type=jnp.float32)
    total_out[...] = part_total[0:8]
    pl.when(outer)(lambda: total_near_copy().start())

    def add_up(step):
        peers(lambda peer: rows_copy(step, peer, peer).wait_recv())
        flat = held[step].reshape(total, width)
        part_sum = jnp.dot(weights[...], flat, preferred_element_type=jnp.float32)

        @pl.when(inner)
        def _():
            sums[step] = part_sum

        @pl.when(outer)
        def _():
            sums_out[step] = part_sum.astype(jnp.bfloat16)
            every_part(lambda part: near_copy(step, part).start())

    def join_totals():
        total_near_copy().wait_recv()
        total_out[...] += total_near[...]
        total_cross_copy().start()

    def join(step, part):
        near_copy(step, part).wait_recv()
        span = cells_of(part)
        joint = sums[step, span] + near_in[step, span].astype(jnp.float32)
        sums[step, span] = joint
        sums_out[step, span] = joint.astype(jnp.bfloat16)
        cross_copy(step, part).start()

    def get_scale():
        total_cross_copy().wait_recv()
        scale_row = 1.0 / jnp.maximum(total_out[0:1] + total_in[0:1], 1.0)
        for c in range(cells // lanes):
            scale[c * lanes : (c + 1) * lanes] = jnp.broadcast_to(
                scale_row[:, c * lanes : (c + 1) * lanes], (lanes, lanes)
            ).T

    def settle(step, part):
        cross_copy(step, part).wait_recv()
        span = cells_of(part)
        whole_sum = sums[step, span] + cross_in[step, span].astype(jnp.float32)
        for k in range(PAIR):
            lane = slice(k * side_len, (k + 1) * side_len)
            templates[step, span, lane] = (whole_sum[:, lane] * scale[span]).astype(jnp.bfloat16)
        back_copy(step, part).start()

    def take_off(step):
        flat = held[step].reshape(total, width)
        chosen = jnp.dot(picks[...], templates[step], preferred_element_type=jnp.float32)
        change = (flat.astype(jnp.float32) - chosen).astype(jnp.bfloat16)
        diffs[step] = change.reshape(PLANE, blocks, width)
        peers(lambda peer: diffs_copy(step, peer, me).start())
        coadd_copy(step).start()
        diffs_in[step, pl.ds(me, 1)] = diffs[step, pl.ds(me, 1)]

    rows_here = CORES * ROWS

    def finish(step):
        start = pl.multiple_of(patch * CELLS, CELLS)
        own = templates[step, pl.ds(start, CELLS)].astype(jnp.float32)
        for k in range(PAIR):
            row = core * ROWS + step * PAIR + k
            coadd_ref[pl.ds(row, CELLS, stride=rows_here), :] = own[:, k * side_len : (k + 1) * side_len]
        peers(lambda peer: diffs_copy(step, peer, peer).wait_recv())

        def spread(source, carry):
            values = diffs_in[step, source].astype(jnp.float32)
            for k in range(PAIR):
                row = source * ROWS + step * PAIR + k
                wide[pl.ds(row, blocks, stride=side_len), :] = values[
                    :, k * side_len : (k + 1) * side_len
                ]
            return carry

        lax.fori_loop(0, PLANE, spread, 0)
        coadd_copy(step).wait_recv()
        other = coadd_in[step].astype(jnp.float32)
        for k in range(PAIR):
            row = (1 - core) * ROWS + step * PAIR + k
            coadd_ref[pl.ds(row, CELLS, stride=rows_here), :] = other[:, k * side_len : (k + 1) * side_len]

    def one_step(step, carry):
        pl.when(step < STEPS)(lambda: add_up(step))
        pl.when(step + ahead < STEPS)(lambda: send_rows_of(step + ahead))

        @pl.when(inner)
        def _():
            pl.when(step == 1)(join_totals)
            pl.when((step >= 1) & (step <= STEPS))(lambda: every_part(lambda part: join(step - 1, part)))
            pl.when(step == 2)(get_scale)
            pl.when((step >= 2) & (step <= STEPS + 1))(lambda: every_part(lambda part: settle(step - 2, part)))

        late = jnp.where(inner, 2, 6)

        @pl.when((step >= late) & (step < STEPS + late))
        def _():
            pl.when(outer)(lambda: every_part(lambda part: back_copy(step - late, part).wait_recv()))
            take_off(step - late)

        last = late + 1
        pl.when((step >= last) & (step < STEPS + last))(lambda: finish(step - last))
        return carry

    lax.fori_loop(0, jnp.where(inner, STEPS + 3, STEPS + 7), one_step, 0)

    def narrow(part, carry):
        start = pl.multiple_of(part * 512, 512)
        difference_ref[pl.ds(start, 512), :] = wide[pl.ds(start, 512), :].astype(jnp.bfloat16)
        return carry

    lax.fori_loop(0, wide.shape[0] // 512, narrow, 0)

    peers(lambda peer: facts_copy(peer, me).wait_send())
    pl.when(inner)(lambda: total_cross_copy().wait_send())
    pl.when(outer)(lambda: total_near_copy().wait_send())

    def sent(step, carry):
        peers(lambda peer: rows_copy(step, peer, me).wait_send())
        peers(lambda peer: diffs_copy(step, peer, me).wait_send())
        coadd_copy(step).wait_send()

        @pl.when(inner)
        def _():
            every_part(lambda part: cross_copy(step, part).wait_send())
            every_part(lambda part: back_copy(step, part).wait_send())

        pl.when(outer)(lambda: every_part(lambda part: near_copy(step, part).wait_send()))
        return carry

    lax.fori_loop(0, STEPS, sent, 0)


def row_shards(pixels, mask_bits, inv_var, owner, cell, coef_index, coef_table):
    blocks, side_len = pixels.shape[0], pixels.shape[1]
    cells = lax.axis_size("patch") * CELLS
    total = PLANE * blocks
    width = PAIR * side_len
    bands = fixed_bands(side_len)
    right_bands = np.transpose(bands, (2, 0, 1)).reshape(side_len, 6 * side_len)
    bf16, f32 = jnp.bfloat16, jnp.float32
    dma = pltpu.SemaphoreType.DMA
    smem, vmem = pl.BlockSpec(memory_space=pltpu.SMEM), pl.BlockSpec(memory_space=pltpu.VMEM)
    coadd, difference = pl.pallas_call(
        trade_kernel,
        in_specs=[smem] * 2 + [vmem] * 5 + [pl.BlockSpec(memory_space=pl.ANY)] * 2,
        out_specs=[vmem] * 2,
        out_shape=[
            jax.ShapeDtypeStruct((CELLS * CORES * ROWS, side_len), f32),
            jax.ShapeDtypeStruct((blocks * side_len, side_len), bf16),
        ],
        scratch_shapes=[
            pltpu.VMEM((blocks, side_len, side_len), bf16),
            pltpu.VMEM((blocks, side_len, side_len), jnp.int32),
            pltpu.VMEM((STEPS, PLANE, blocks, width), bf16),
            pltpu.VMEM((STEPS, PLANE, blocks, width), bf16),
            pltpu.VMEM((STEPS, cells, width), f32),
            pltpu.VMEM((STEPS, cells, width), bf16),
            pltpu.VMEM((STEPS, cells, width), bf16),
            pltpu.VMEM((STEPS, cells, width), bf16),
            pltpu.VMEM((STEPS, cells, width), bf16),
            pltpu.VMEM((STEPS, CELLS, width), bf16),
            pltpu.VMEM((STEPS, PLANE, blocks, width), bf16),
            pltpu.VMEM((STEPS, PLANE, blocks, width), bf16),
            pltpu.VMEM((cells, total), bf16),
            pltpu.VMEM((total, cells), bf16),
            pltpu.VMEM((blocks * side_len, side_len), f32),
            pltpu.VMEM((8, 2 * blocks), f32),
            pltpu.VMEM((PLANE, 8, 2 * blocks), f32),
            pltpu.VMEM((16, total), bf16),
            pltpu.VMEM((8, cells), f32),
            pltpu.VMEM((8, cells), f32),
            pltpu.VMEM((8, cells), f32),
            pltpu.VMEM((cells, side_len), f32),
            dma((LOADS,)),
            dma((LOADS,)),
            dma((STEPS, PLANE)),
            dma((STEPS, PLANE)),
            dma((PLANE,)),
            dma((PLANE,)),
            dma,
            dma,
            dma,
        ]
        + [dma((STEPS, PARTS))] * 6
        + [dma((STEPS,))] * 2
        + [dma((STEPS, PLANE))] * 2,
        compiler_params=pltpu.CompilerParams(
            collective_id=0, has_side_effects=True, vmem_limit_bytes=58 * 2**20
        ),
    )(
        coef_index, coef_table.T,
        inv_var.reshape(1, blocks), owner.reshape(1, blocks), cell.reshape(1, blocks),
        jnp.asarray(right_bands, dtype=bf16), jnp.asarray(bands), pixels, mask_bits,
    )
    return (
        coadd.reshape(CELLS, CORES * ROWS, side_len),
        difference.reshape(blocks, side_len, side_len),
    )


def solution(mesh):
    placed = (
        P(("visit", "patch"), None, None),
        P(("visit", "patch"), None, None),
        P(("visit", "patch")),
        P(("visit", "patch")),
        P(("visit", "patch")),
        P(("visit", "patch")),
        P(),
    )
    fits = mesh.shape["visit"] * CORES == PLANE and mesh.shape["patch"] == 4 * CORES
    return jax.shard_map(
        row_shards if fits else shards,
        mesh=mesh,
        in_specs=placed,
        out_specs=(P("patch", "visit", None), P(("visit", "patch"), None, None)),
        check_vma=False,
    )
```

```python
import jax
import jax.numpy as jnp
import numpy as np
from jax import lax
from jax.experimental import pallas as pl
from jax.experimental.pallas import tpu as pltpu
from jax.sharding import PartitionSpec as P

CELLS = 64
KSIZE = 21


gauss_widths = (1.0, 2.0, 3.5)


def band_tables(side_len):
    tap_reach = KSIZE // 2
    position = jnp.arange(side_len).astype(jnp.float32)
    offset = position[:, None] - position[None, :]
    inside = jnp.abs(offset) <= tap_reach
    tap_offsets = jnp.arange(-tap_reach, tap_reach + 1).astype(jnp.float32)
    tables = []
    for spread in gauss_widths:
        profile_sum = jnp.sum(jnp.exp(-tap_offsets * tap_offsets / (2.0 * spread * spread)))
        even_band = jnp.where(
            inside, jnp.exp(-offset * offset / (2.0 * spread * spread)) / profile_sum, 0.0
        )
        tables.append(even_band)
        tables.append(even_band * offset / spread)
    return jnp.stack(tables)


def match_group(blocks, coefficients, tables, right_bands):
    number = blocks.shape[0]
    side_len = blocks.shape[1]
    columns = jnp.dot(
        blocks.reshape(number * side_len, side_len), right_bands, preferred_element_type=jnp.float32
    )
    columns = columns.astype(jnp.bfloat16).reshape(number, side_len, 6, side_len)
    left_parts = []
    for sigma_pos in range(3):
        even_band = tables[2 * sigma_pos]
        odd_band = tables[2 * sigma_pos + 1]
        left_parts.append(
            coefficients[:, 3 * sigma_pos, None, None] * even_band
            + coefficients[:, 3 * sigma_pos + 1, None, None] * odd_band
        )
        left_parts.append(coefficients[:, 3 * sigma_pos + 2, None, None] * even_band)
    left_bands = jnp.stack(left_parts, axis=2).astype(jnp.bfloat16)
    result = jnp.einsum("nisp,npsj->nij", left_bands, columns, preferred_element_type=jnp.float32)
    return result.astype(jnp.bfloat16)


def match_blocks(blocks, coefficients, tables, right_bands):
    number = blocks.shape[0]
    side_len = blocks.shape[1]
    batch_blocks = 16
    rounds = -(-number // batch_blocks)

    def one_batch(bundle):
        return match_group(bundle[0], bundle[1], tables, right_bands)

    matched = lax.map(
        one_batch,
        (
            blocks.reshape(rounds, batch_blocks, side_len, side_len),
            coefficients.reshape(rounds, batch_blocks, coefficients.shape[1]),
        ),
    )
    return matched.reshape(rounds * batch_blocks, side_len, side_len)[:number]


def shards(pixels, mask_bits, inv_var, owner, cell, coef_index, coef_table):
    blocks_here = pixels.shape[0]
    side_len = pixels.shape[1]
    kernel_sets = coef_table.shape[0]
    patches = lax.axis_size("patch")
    visits = lax.axis_size("visit")
    capacity = 4 * blocks_here // patches
    slot_total = patches * capacity
    tables = band_tables(side_len)
    right_bands = (
        jnp.transpose(tables, (2, 0, 1)).reshape(side_len, 6 * side_len).astype(jnp.bfloat16)
    )
    usable = (mask_bits % 2 == 0) & (mask_bits // 2 % 2 == 0) & (mask_bits // 4 % 2 == 0)
    masked = jnp.where(usable, pixels, jnp.zeros((), jnp.bfloat16))
    weight = inv_var.astype(jnp.bfloat16)
    cell_weight = jnp.where(
        cell[:, None] == jnp.arange(CELLS)[None, :], weight[:, None], jnp.zeros((), jnp.bfloat16)
    )
    chosen = (coef_index[:, None] == jnp.arange(kernel_sets)[None, :]).astype(jnp.bfloat16)
    dest_onehot = (owner[:, None] == jnp.arange(patches)[None, :]).astype(jnp.int32)
    slot_rank = jnp.sum((jnp.cumsum(dest_onehot, axis=0) - dest_onehot) * dest_onehot, axis=1)
    slot_of_block = owner * capacity + slot_rank
    matches = slot_of_block[None, :] == jnp.arange(slot_total)[:, None]
    source_row = jnp.sum(jnp.where(matches, jnp.arange(blocks_here)[None, :], 0), axis=1)
    filled = jnp.any(matches, axis=1)

    def pack_slots(values):
        picked = values[source_row]
        keep_rows = filled.reshape((slot_total,) + (1,) * (values.ndim - 1))
        picked = jnp.where(keep_rows, picked, jnp.zeros((), values.dtype))
        return picked.reshape((patches, capacity) + values.shape[1:])

    pieces = lax.all_to_all(pack_slots(masked), "patch", split_axis=0, concat_axis=0, tiled=True)
    weights = lax.all_to_all(
        pack_slots(cell_weight), "patch", split_axis=0, concat_axis=0, tiled=True
    )
    kernel_picks = lax.all_to_all(
        pack_slots(chosen), "patch", split_axis=0, concat_axis=0, tiled=True
    )
    flat_blocks = pieces.reshape((-1, side_len, side_len))
    coefficients = jnp.dot(
        kernel_picks.reshape(-1, kernel_sets).astype(jnp.float32),
        coef_table,
        precision=lax.Precision.HIGHEST,
    )
    matched = match_blocks(flat_blocks, coefficients, tables, right_bands)
    matched_slots = matched.reshape(pieces.shape)
    flat_weights = weights.reshape(slot_total, CELLS)
    flat_matched = matched_slots.reshape(slot_total, side_len * side_len)
    numerator = jnp.einsum(
        "sc,sk->ck", flat_weights, flat_matched, preferred_element_type=jnp.float32
    ).reshape(CELLS, side_len, side_len)
    weight_sum = jnp.sum(flat_weights.astype(jnp.float32), axis=0)
    rows_here = side_len // visits
    numerator, weight_sum = lax.psum((numerator, weight_sum), "visit")
    coadd_full = numerator / jnp.maximum(weight_sum, 1.0)[:, None, None]
    coadd_part = lax.dynamic_slice_in_dim(
        coadd_full, lax.axis_index("visit") * rows_here, rows_here, 1
    )
    template = coadd_full.astype(jnp.bfloat16)
    live_slots = (flat_weights > 0).astype(jnp.bfloat16)
    slot_template = jnp.einsum(
        "sc,ck->sk",
        live_slots,
        template.reshape(CELLS, side_len * side_len),
        preferred_element_type=jnp.float32,
    )
    difference_slots = (flat_matched.astype(jnp.float32) - slot_template).astype(jnp.bfloat16)
    returned = lax.all_to_all(
        difference_slots.reshape(patches, capacity, side_len, side_len),
        "patch",
        split_axis=0,
        concat_axis=0,
        tiled=True,
    )
    difference = returned.reshape(slot_total, side_len, side_len)[slot_of_block]
    return (coadd_part, difference)


PLANE = 8
CORES = 2
ROWS = 16
STEPS = 4
PAIR = ROWS // STEPS
LOADS = 4
PARTS = 4
MESH = pl.DeviceIdType.MESH


def fixed_bands(side_len):
    reach = KSIZE // 2
    position = np.arange(side_len, dtype=np.float32)
    offset = position[:, None] - position[None, :]
    taps = np.arange(-reach, reach + 1).astype(np.float32)
    tables = []
    for spread in gauss_widths:
        spread = np.float32(spread)
        total = np.sum(np.exp(-taps * taps / (2 * spread * spread)))
        even = np.where(np.abs(offset) <= reach, np.exp(-offset * offset / (2 * spread * spread)) / total, 0)
        tables.append(even.astype(np.float32))
        tables.append((even * offset / spread).astype(np.float32))
    return np.stack(tables)


def trade_kernel(
    index_ref, table_ref, inv_var_ref, owner_ref, cell_ref, right_ref, bands_ref, pixels_hbm, mask_hbm,
    coadd_ref, difference_ref,
    pixels, mask, rows, held, sums, sums_out, near_in, cross_in, templates, coadd_in, diffs, diffs_in,
    weights, picks, wide, facts, facts_in, weight_rows, total_out, total_near, total_in, scale,
    load_pixels, load_mask, send_rows, recv_rows, send_facts, recv_facts,
    send_total, recv_total_near, recv_total_cross, send_near, recv_near, send_cross, recv_cross,
    send_back, recv_back, send_coadd, recv_coadd, send_diffs, recv_diffs,
):
    blocks, side_len = pixels.shape[0], pixels.shape[1]
    total = PLANE * blocks
    cells = weights.shape[0]
    width = PAIR * side_len
    lanes = 2 * blocks
    load = blocks // LOADS
    visit, patch = lax.axis_index("visit"), lax.axis_index("patch")
    layer, core = patch // CORES, patch % CORES
    me = visit * CORES + core
    inner = (layer + 1) // 2 == 1
    outer = jnp.logical_not(inner)
    mate = (visit, (layer + 1 - 2 * (layer % 2)) * CORES + core)
    across = (visit, (3 - layer) * CORES + core)
    barrier = pltpu.get_barrier_semaphore()

    def device_of(index):
        return (index // CORES, layer * CORES + index % CORES)

    def peers(act):
        def one(turn, carry):
            act((me + turn) % PLANE)
            return carry

        lax.fori_loop(1, PLANE, one, 0)

    def greet(device):
        pl.semaphore_signal(barrier, inc=1, device_id=device, device_id_type=MESH)

    def load_copies(part):
        span = pl.ds(part * load, load)
        return (
            pltpu.make_async_copy(pixels_hbm.at[span], pixels.at[span], load_pixels.at[part]),
            pltpu.make_async_copy(mask_hbm.at[span], mask.at[span], load_mask.at[part]),
        )

    def send(source, target, send_sem, recv_sem, device):
        return pltpu.make_async_remote_copy(
            src_ref=source, dst_ref=target, send_sem=send_sem, recv_sem=recv_sem,
            device_id=device, device_id_type=MESH,
        )

    def facts_copy(peer, slot):
        return send(facts, facts_in.at[slot], send_facts.at[peer], recv_facts.at[slot], device_of(peer))

    def rows_copy(step, peer, slot):
        return send(
            rows.at[step, peer], held.at[step, slot],
            send_rows.at[step, peer], recv_rows.at[step, slot], device_of(peer),
        )

    def total_near_copy():
        return send(total_out, total_near, send_total, recv_total_near, mate)

    def total_cross_copy():
        return send(total_out, total_in, send_total, recv_total_cross, across)

    some = cells // PARTS

    def cells_of(part):
        return pl.ds(pl.multiple_of(part * some, some), some)

    def every_part(act):
        def one(part, carry):
            act(part)
            return carry

        lax.fori_loop(0, PARTS, one, 0)

    def near_copy(step, part):
        span = cells_of(part)
        return send(
            sums_out.at[step, span], near_in.at[step, span],
            send_near.at[step, part], recv_near.at[step, part], mate,
        )

    def cross_copy(step, part):
        span = cells_of(part)
        return send(
            sums_out.at[step, span], cross_in.at[step, span],
            send_cross.at[step, part], recv_cross.at[step, part], across,
        )

    def back_copy(step, part):
        span = cells_of(part)
        return send(
            templates.at[step, span], templates.at[step, span],
            send_back.at[step, part], recv_back.at[step, part], mate,
        )

    def coadd_copy(step):
        start = pl.multiple_of((layer * CORES + 1 - core) * CELLS, CELLS)
        return send(
            templates.at[step, pl.ds(start, CELLS)], coadd_in.at[step],
            send_coadd.at[step], recv_coadd.at[step], (visit, layer * CORES + 1 - core),
        )

    def diffs_copy(step, peer, slot):
        return send(
            diffs.at[step, peer], diffs_in.at[step, slot],
            send_diffs.at[step, peer], recv_diffs.at[step, slot], device_of(peer),
        )

    for part in range(LOADS):
        for copy in load_copies(part):
            copy.start()

    peers(lambda peer: greet(device_of(peer)))
    greet(mate)
    pl.when(inner)(lambda: greet(across))

    segment = (owner_ref[...] * CELLS + cell_ref[...]).astype(jnp.float32)
    weight = inv_var_ref[...].astype(jnp.bfloat16).astype(jnp.float32)
    facts[...] = jnp.zeros_like(facts)
    facts[0:1, :] = jnp.concatenate([segment, segment], axis=1)
    facts[1:2, :] = jnp.concatenate([weight, weight], axis=1)

    unit = 4

    def match_unit(part, carry):
        first = part * unit
        usable = (mask[pl.ds(first, unit)] & 7) == 0
        masked = jnp.where(usable, pixels[pl.ds(first, unit)].astype(jnp.float32), 0.0)
        masked = masked.astype(jnp.bfloat16).reshape(unit * side_len, side_len)
        columns = jnp.dot(masked, right_ref[...], preferred_element_type=jnp.float32)
        columns = columns.astype(jnp.bfloat16)
        for n in range(unit):
            kernel_set = index_ref[first + n]
            left_parts = []
            for m in range(3):
                even, odd = bands_ref[2 * m], bands_ref[2 * m + 1]
                coef = [table_ref[3 * m + t, kernel_set] for t in range(3)]
                left_parts.append((coef[0] * even + coef[1] * odd).astype(jnp.bfloat16))
                left_parts.append((coef[2] * even).astype(jnp.bfloat16))
            left = jnp.concatenate(left_parts, axis=1)
            own = columns[n * side_len : (n + 1) * side_len]
            stacked = jnp.concatenate(
                [own[:, p * side_len : (p + 1) * side_len] for p in range(6)], axis=0
            )
            start = pl.multiple_of((first + n) * side_len, side_len)
            wide[pl.ds(start, side_len), :] = jnp.dot(left, stacked, preferred_element_type=jnp.float32)
        return carry

    for part in range(LOADS):
        for copy in load_copies(part):
            copy.wait()
        lax.fori_loop(part * load // unit, (part + 1) * load // unit, match_unit, 0)

    pl.semaphore_wait(barrier, jnp.where(inner, PLANE + 1, PLANE))
    peers(lambda peer: facts_copy(peer, me).start())

    def send_rows_of(step):
        def gather_rows(peer, carry):
            for k in range(PAIR):
                start = peer * ROWS + step * PAIR + k
                values = wide[pl.ds(start, blocks, stride=side_len), :].astype(jnp.bfloat16)
                rows[step, peer, :, k * side_len : (k + 1) * side_len] = values
            return carry

        lax.fori_loop(0, PLANE, gather_rows, 0)
        peers(lambda peer: rows_copy(step, peer, me).start())
        held[step, pl.ds(me, 1)] = rows[step, pl.ds(me, 1)]

    ahead = 2
    for step in range(ahead):
        send_rows_of(step)
    facts_in[pl.ds(me, 1)] = facts[...].reshape((1,) + facts.shape)
    peers(lambda peer: facts_copy(peer, peer).wait_recv())

    def make_pickers(pair, carry):
        first_lanes = lax.broadcasted_iota(jnp.int32, (1, lanes), 1) < blocks
        segment = jnp.where(first_lanes, facts_in[2 * pair, 0:1, :], facts_in[2 * pair + 1, 0:1, :])
        weight = jnp.where(first_lanes, facts_in[2 * pair, 1:2, :], facts_in[2 * pair + 1, 1:2, :])
        start = pl.multiple_of(pair * lanes, lanes)
        cell = lax.broadcasted_iota(jnp.int32, (cells, lanes), 0).astype(jnp.float32)
        weights[:, pl.ds(start, lanes)] = jnp.where(cell == segment, weight, 0.0).astype(jnp.bfloat16)
        weight_rows[:, pl.ds(start, lanes)] = jnp.broadcast_to(weight, (16, lanes)).astype(jnp.bfloat16)
        segment_column = jnp.broadcast_to(segment, (lanes, lanes)).T
        for c in range(cells // lanes):
            cell = lax.broadcasted_iota(jnp.int32, (lanes, lanes), 1) + c * lanes
            chosen = jnp.where(cell.astype(jnp.float32) == segment_column, 1.0, 0.0)
            picks[pl.ds(start, lanes), c * lanes : (c + 1) * lanes] = chosen.astype(jnp.bfloat16)
        return carry

    lax.fori_loop(0, PLANE // 2, make_pickers, 0)
    part_total = jnp.dot(weight_rows[...], picks[...], preferred_element_type=jnp.float32)
    total_out[...] = part_total[0:8]
    pl.when(outer)(lambda: total_near_copy().start())

    def add_up(step):
        peers(lambda peer: rows_copy(step, peer, peer).wait_recv())
        flat = held[step].reshape(total, width)
        part_sum = jnp.dot(weights[...], flat, preferred_element_type=jnp.float32)

        @pl.when(inner)
        def _():
            sums[step] = part_sum

        @pl.when(outer)
        def _():
            sums_out[step] = part_sum.astype(jnp.bfloat16)
            every_part(lambda part: near_copy(step, part).start())

    def join_totals():
        total_near_copy().wait_recv()
        total_out[...] += total_near[...]
        total_cross_copy().start()

    def join(step, part):
        near_copy(step, part).wait_recv()
        span = cells_of(part)
        joint = sums[step, span] + near_in[step, span].astype(jnp.float32)
        sums[step, span] = joint
        sums_out[step, span] = joint.astype(jnp.bfloat16)
        cross_copy(step, part).start()

    def get_scale():
        total_cross_copy().wait_recv()
        scale_row = 1.0 / jnp.maximum(total_out[0:1] + total_in[0:1], 1.0)
        for c in range(cells // lanes):
            scale[c * lanes : (c + 1) * lanes] = jnp.broadcast_to(
                scale_row[:, c * lanes : (c + 1) * lanes], (lanes, lanes)
            ).T

    def settle(step, part):
        cross_copy(step, part).wait_recv()
        span = cells_of(part)
        whole_sum = sums[step, span] + cross_in[step, span].astype(jnp.float32)
        for k in range(PAIR):
            lane = slice(k * side_len, (k + 1) * side_len)
            templates[step, span, lane] = (whole_sum[:, lane] * scale[span]).astype(jnp.bfloat16)
        back_copy(step, part).start()

    def take_off(step):
        flat = held[step].reshape(total, width)
        chosen = jnp.dot(picks[...], templates[step], preferred_element_type=jnp.float32)
        change = (flat.astype(jnp.float32) - chosen).astype(jnp.bfloat16)
        diffs[step] = change.reshape(PLANE, blocks, width)
        peers(lambda peer: diffs_copy(step, peer, me).start())
        coadd_copy(step).start()
        diffs_in[step, pl.ds(me, 1)] = diffs[step, pl.ds(me, 1)]

    rows_here = CORES * ROWS

    def finish(step):
        start = pl.multiple_of(patch * CELLS, CELLS)
        own = templates[step, pl.ds(start, CELLS)].astype(jnp.float32)
        for k in range(PAIR):
            row = core * ROWS + step * PAIR + k
            coadd_ref[pl.ds(row, CELLS, stride=rows_here), :] = own[:, k * side_len : (k + 1) * side_len]
        peers(lambda peer: diffs_copy(step, peer, peer).wait_recv())

        def spread(source, carry):
            values = diffs_in[step, source].astype(jnp.float32)
            for k in range(PAIR):
                row = source * ROWS + step * PAIR + k
                wide[pl.ds(row, blocks, stride=side_len), :] = values[
                    :, k * side_len : (k + 1) * side_len
                ]
            return carry

        lax.fori_loop(0, PLANE, spread, 0)
        coadd_copy(step).wait_recv()
        other = coadd_in[step].astype(jnp.float32)
        for k in range(PAIR):
            row = (1 - core) * ROWS + step * PAIR + k
            coadd_ref[pl.ds(row, CELLS, stride=rows_here), :] = other[:, k * side_len : (k + 1) * side_len]

    def one_step(step, carry):
        @pl.when(inner)
        def _():
            pl.when(step == 1)(join_totals)
            pl.when((step >= 1) & (step <= STEPS))(lambda: every_part(lambda part: join(step - 1, part)))
            pl.when(step == 2)(get_scale)
            pl.when((step >= 2) & (step <= STEPS + 1))(lambda: every_part(lambda part: settle(step - 2, part)))

        pl.when(step < STEPS)(lambda: add_up(step))
        pl.when(step + ahead < STEPS)(lambda: send_rows_of(step + ahead))

        late = jnp.where(inner, 2, 4)

        @pl.when((step >= late) & (step < STEPS + late))
        def _():
            pl.when(outer)(lambda: every_part(lambda part: back_copy(step - late, part).wait_recv()))
            take_off(step - late)

        last = late + 1
        pl.when((step >= last) & (step < STEPS + last))(lambda: finish(step - last))
        return carry

    lax.fori_loop(0, jnp.where(inner, STEPS + 3, STEPS + 5), one_step, 0)

    def narrow(part, carry):
        start = pl.multiple_of(part * 512, 512)
        difference_ref[pl.ds(start, 512), :] = wide[pl.ds(start, 512), :].astype(jnp.bfloat16)
        return carry

    lax.fori_loop(0, wide.shape[0] // 512, narrow, 0)

    peers(lambda peer: facts_copy(peer, me).wait_send())
    pl.when(inner)(lambda: total_cross_copy().wait_send())
    pl.when(outer)(lambda: total_near_copy().wait_send())

    def sent(step, carry):
        peers(lambda peer: rows_copy(step, peer, me).wait_send())
        peers(lambda peer: diffs_copy(step, peer, me).wait_send())
        coadd_copy(step).wait_send()

        @pl.when(inner)
        def _():
            every_part(lambda part: cross_copy(step, part).wait_send())
            every_part(lambda part: back_copy(step, part).wait_send())

        pl.when(outer)(lambda: every_part(lambda part: near_copy(step, part).wait_send()))
        return carry

    lax.fori_loop(0, STEPS, sent, 0)


def row_shards(pixels, mask_bits, inv_var, owner, cell, coef_index, coef_table):
    blocks, side_len = pixels.shape[0], pixels.shape[1]
    cells = lax.axis_size("patch") * CELLS
    total = PLANE * blocks
    width = PAIR * side_len
    bands = fixed_bands(side_len)
    right_bands = np.transpose(bands, (2, 0, 1)).reshape(side_len, 6 * side_len)
    bf16, f32 = jnp.bfloat16, jnp.float32
    dma = pltpu.SemaphoreType.DMA
    smem, vmem = pl.BlockSpec(memory_space=pltpu.SMEM), pl.BlockSpec(memory_space=pltpu.VMEM)
    coadd, difference = pl.pallas_call(
        trade_kernel,
        in_specs=[smem] * 2 + [vmem] * 5 + [pl.BlockSpec(memory_space=pl.ANY)] * 2,
        out_specs=[vmem] * 2,
        out_shape=[
            jax.ShapeDtypeStruct((CELLS * CORES * ROWS, side_len), f32),
            jax.ShapeDtypeStruct((blocks * side_len, side_len), bf16),
        ],
        scratch_shapes=[
            pltpu.VMEM((blocks, side_len, side_len), bf16),
            pltpu.VMEM((blocks, side_len, side_len), jnp.int32),
            pltpu.VMEM((STEPS, PLANE, blocks, width), bf16),
            pltpu.VMEM((STEPS, PLANE, blocks, width), bf16),
            pltpu.VMEM((STEPS, cells, width), f32),
            pltpu.VMEM((STEPS, cells, width), bf16),
            pltpu.VMEM((STEPS, cells, width), bf16),
            pltpu.VMEM((STEPS, cells, width), bf16),
            pltpu.VMEM((STEPS, cells, width), bf16),
            pltpu.VMEM((STEPS, CELLS, width), bf16),
            pltpu.VMEM((STEPS, PLANE, blocks, width), bf16),
            pltpu.VMEM((STEPS, PLANE, blocks, width), bf16),
            pltpu.VMEM((cells, total), bf16),
            pltpu.VMEM((total, cells), bf16),
            pltpu.VMEM((blocks * side_len, side_len), f32),
            pltpu.VMEM((8, 2 * blocks), f32),
            pltpu.VMEM((PLANE, 8, 2 * blocks), f32),
            pltpu.VMEM((16, total), bf16),
            pltpu.VMEM((8, cells), f32),
            pltpu.VMEM((8, cells), f32),
            pltpu.VMEM((8, cells), f32),
            pltpu.VMEM((cells, side_len), f32),
            dma((LOADS,)),
            dma((LOADS,)),
            dma((STEPS, PLANE)),
            dma((STEPS, PLANE)),
            dma((PLANE,)),
            dma((PLANE,)),
            dma,
            dma,
            dma,
        ]
        + [dma((STEPS, PARTS))] * 6
        + [dma((STEPS,))] * 2
        + [dma((STEPS, PLANE))] * 2,
        compiler_params=pltpu.CompilerParams(
            collective_id=0, has_side_effects=True, vmem_limit_bytes=58 * 2**20
        ),
    )(
        coef_index, coef_table.T,
        inv_var.reshape(1, blocks), owner.reshape(1, blocks), cell.reshape(1, blocks),
        jnp.asarray(right_bands, dtype=bf16), jnp.asarray(bands), pixels, mask_bits,
    )
    return (
        coadd.reshape(CELLS, CORES * ROWS, side_len),
        difference.reshape(blocks, side_len, side_len),
    )


def solution(mesh):
    placed = (
        P(("visit", "patch"), None, None),
        P(("visit", "patch"), None, None),
        P(("visit", "patch")),
        P(("visit", "patch")),
        P(("visit", "patch")),
        P(("visit", "patch")),
        P(),
    )
    fits = mesh.shape["visit"] * CORES == PLANE and mesh.shape["patch"] == 4 * CORES
    return jax.shard_map(
        row_shards if fits else shards,
        mesh=mesh,
        in_specs=placed,
        out_specs=(P("patch", "visit", None), P(("visit", "patch"), None, None)),
        check_vma=False,
    )
```

```python
import jax
import jax.numpy as jnp
import numpy as np
from jax import lax
from jax.experimental import pallas as pl
from jax.experimental.pallas import tpu as pltpu
from jax.sharding import PartitionSpec as P

CELLS = 64
KSIZE = 21


gauss_widths = (1.0, 2.0, 3.5)


def band_tables(side_len):
    tap_reach = KSIZE // 2
    position = jnp.arange(side_len).astype(jnp.float32)
    offset = position[:, None] - position[None, :]
    inside = jnp.abs(offset) <= tap_reach
    tap_offsets = jnp.arange(-tap_reach, tap_reach + 1).astype(jnp.float32)
    tables = []
    for spread in gauss_widths:
        profile_sum = jnp.sum(jnp.exp(-tap_offsets * tap_offsets / (2.0 * spread * spread)))
        even_band = jnp.where(
            inside, jnp.exp(-offset * offset / (2.0 * spread * spread)) / profile_sum, 0.0
        )
        tables.append(even_band)
        tables.append(even_band * offset / spread)
    return jnp.stack(tables)


def match_group(blocks, coefficients, tables, right_bands):
    number = blocks.shape[0]
    side_len = blocks.shape[1]
    columns = jnp.dot(
        blocks.reshape(number * side_len, side_len), right_bands, preferred_element_type=jnp.float32
    )
    columns = columns.astype(jnp.bfloat16).reshape(number, side_len, 6, side_len)
    left_parts = []
    for sigma_pos in range(3):
        even_band = tables[2 * sigma_pos]
        odd_band = tables[2 * sigma_pos + 1]
        left_parts.append(
            coefficients[:, 3 * sigma_pos, None, None] * even_band
            + coefficients[:, 3 * sigma_pos + 1, None, None] * odd_band
        )
        left_parts.append(coefficients[:, 3 * sigma_pos + 2, None, None] * even_band)
    left_bands = jnp.stack(left_parts, axis=2).astype(jnp.bfloat16)
    result = jnp.einsum("nisp,npsj->nij", left_bands, columns, preferred_element_type=jnp.float32)
    return result.astype(jnp.bfloat16)


def match_blocks(blocks, coefficients, tables, right_bands):
    number = blocks.shape[0]
    side_len = blocks.shape[1]
    batch_blocks = 16
    rounds = -(-number // batch_blocks)

    def one_batch(bundle):
        return match_group(bundle[0], bundle[1], tables, right_bands)

    matched = lax.map(
        one_batch,
        (
            blocks.reshape(rounds, batch_blocks, side_len, side_len),
            coefficients.reshape(rounds, batch_blocks, coefficients.shape[1]),
        ),
    )
    return matched.reshape(rounds * batch_blocks, side_len, side_len)[:number]


def shards(pixels, mask_bits, inv_var, owner, cell, coef_index, coef_table):
    blocks_here = pixels.shape[0]
    side_len = pixels.shape[1]
    kernel_sets = coef_table.shape[0]
    patches = lax.axis_size("patch")
    visits = lax.axis_size("visit")
    capacity = 4 * blocks_here // patches
    slot_total = patches * capacity
    tables = band_tables(side_len)
    right_bands = (
        jnp.transpose(tables, (2, 0, 1)).reshape(side_len, 6 * side_len).astype(jnp.bfloat16)
    )
    usable = (mask_bits % 2 == 0) & (mask_bits // 2 % 2 == 0) & (mask_bits // 4 % 2 == 0)
    masked = jnp.where(usable, pixels, jnp.zeros((), jnp.bfloat16))
    weight = inv_var.astype(jnp.bfloat16)
    cell_weight = jnp.where(
        cell[:, None] == jnp.arange(CELLS)[None, :], weight[:, None], jnp.zeros((), jnp.bfloat16)
    )
    chosen = (coef_index[:, None] == jnp.arange(kernel_sets)[None, :]).astype(jnp.bfloat16)
    dest_onehot = (owner[:, None] == jnp.arange(patches)[None, :]).astype(jnp.int32)
    slot_rank = jnp.sum((jnp.cumsum(dest_onehot, axis=0) - dest_onehot) * dest_onehot, axis=1)
    slot_of_block = owner * capacity + slot_rank
    matches = slot_of_block[None, :] == jnp.arange(slot_total)[:, None]
    source_row = jnp.sum(jnp.where(matches, jnp.arange(blocks_here)[None, :], 0), axis=1)
    filled = jnp.any(matches, axis=1)

    def pack_slots(values):
        picked = values[source_row]
        keep_rows = filled.reshape((slot_total,) + (1,) * (values.ndim - 1))
        picked = jnp.where(keep_rows, picked, jnp.zeros((), values.dtype))
        return picked.reshape((patches, capacity) + values.shape[1:])

    pieces = lax.all_to_all(pack_slots(masked), "patch", split_axis=0, concat_axis=0, tiled=True)
    weights = lax.all_to_all(
        pack_slots(cell_weight), "patch", split_axis=0, concat_axis=0, tiled=True
    )
    kernel_picks = lax.all_to_all(
        pack_slots(chosen), "patch", split_axis=0, concat_axis=0, tiled=True
    )
    flat_blocks = pieces.reshape((-1, side_len, side_len))
    coefficients = jnp.dot(
        kernel_picks.reshape(-1, kernel_sets).astype(jnp.float32),
        coef_table,
        precision=lax.Precision.HIGHEST,
    )
    matched = match_blocks(flat_blocks, coefficients, tables, right_bands)
    matched_slots = matched.reshape(pieces.shape)
    flat_weights = weights.reshape(slot_total, CELLS)
    flat_matched = matched_slots.reshape(slot_total, side_len * side_len)
    numerator = jnp.einsum(
        "sc,sk->ck", flat_weights, flat_matched, preferred_element_type=jnp.float32
    ).reshape(CELLS, side_len, side_len)
    weight_sum = jnp.sum(flat_weights.astype(jnp.float32), axis=0)
    rows_here = side_len // visits
    numerator, weight_sum = lax.psum((numerator, weight_sum), "visit")
    coadd_full = numerator / jnp.maximum(weight_sum, 1.0)[:, None, None]
    coadd_part = lax.dynamic_slice_in_dim(
        coadd_full, lax.axis_index("visit") * rows_here, rows_here, 1
    )
    template = coadd_full.astype(jnp.bfloat16)
    live_slots = (flat_weights > 0).astype(jnp.bfloat16)
    slot_template = jnp.einsum(
        "sc,ck->sk",
        live_slots,
        template.reshape(CELLS, side_len * side_len),
        preferred_element_type=jnp.float32,
    )
    difference_slots = (flat_matched.astype(jnp.float32) - slot_template).astype(jnp.bfloat16)
    returned = lax.all_to_all(
        difference_slots.reshape(patches, capacity, side_len, side_len),
        "patch",
        split_axis=0,
        concat_axis=0,
        tiled=True,
    )
    difference = returned.reshape(slot_total, side_len, side_len)[slot_of_block]
    return (coadd_part, difference)


PLANE = 8
CORES = 2
ROWS = 16
STEPS = 16
PAIR = ROWS // STEPS
LOADS = 4
PARTS = 2
MESH = pl.DeviceIdType.MESH


def fixed_bands(side_len):
    reach = KSIZE // 2
    position = np.arange(side_len, dtype=np.float32)
    offset = position[:, None] - position[None, :]
    taps = np.arange(-reach, reach + 1).astype(np.float32)
    tables = []
    for spread in gauss_widths:
        spread = np.float32(spread)
        total = np.sum(np.exp(-taps * taps / (2 * spread * spread)))
        even = np.where(np.abs(offset) <= reach, np.exp(-offset * offset / (2 * spread * spread)) / total, 0)
        tables.append(even.astype(np.float32))
        tables.append((even * offset / spread).astype(np.float32))
    return np.stack(tables)


def trade_kernel(
    index_ref, table_ref, inv_var_ref, owner_ref, cell_ref, right_ref, bands_ref, pixels_hbm, mask_hbm,
    coadd_ref, difference_ref,
    pixels, mask, rows, held, sums, sums_out, near_in, cross_in, templates, coadd_in, diffs, diffs_in,
    weights, picks, wide, facts, facts_in, weight_rows, total_out, total_near, total_in, scale,
    load_pixels, load_mask, send_rows, recv_rows, send_facts, recv_facts,
    send_total, recv_total_near, recv_total_cross, send_near, recv_near, send_cross, recv_cross,
    send_back, recv_back, send_coadd, recv_coadd, send_diffs, recv_diffs,
):
    blocks, side_len = pixels.shape[0], pixels.shape[1]
    total = PLANE * blocks
    cells = weights.shape[0]
    width = PAIR * side_len
    lanes = 2 * blocks
    load = blocks // LOADS
    visit, patch = lax.axis_index("visit"), lax.axis_index("patch")
    layer, core = patch // CORES, patch % CORES
    me = visit * CORES + core
    inner = (layer + 1) // 2 == 1
    outer = jnp.logical_not(inner)
    mate = (visit, (layer + 1 - 2 * (layer % 2)) * CORES + core)
    across = (visit, (3 - layer) * CORES + core)
    barrier = pltpu.get_barrier_semaphore()

    def device_of(index):
        return (index // CORES, layer * CORES + index % CORES)

    def peers(act):
        def one(turn, carry):
            act((me + turn) % PLANE)
            return carry

        lax.fori_loop(1, PLANE, one, 0)

    def greet(device):
        pl.semaphore_signal(barrier, inc=1, device_id=device, device_id_type=MESH)

    def load_copies(part):
        span = pl.ds(part * load, load)
        return (
            pltpu.make_async_copy(pixels_hbm.at[span], pixels.at[span], load_pixels.at[part]),
            pltpu.make_async_copy(mask_hbm.at[span], mask.at[span], load_mask.at[part]),
        )

    def send(source, target, send_sem, recv_sem, device):
        return pltpu.make_async_remote_copy(
            src_ref=source, dst_ref=target, send_sem=send_sem, recv_sem=recv_sem,
            device_id=device, device_id_type=MESH,
        )

    def facts_copy(peer, slot):
        return send(facts, facts_in.at[slot], send_facts.at[peer], recv_facts.at[slot], device_of(peer))

    def rows_copy(step, peer, slot):
        return send(
            rows.at[step, peer], held.at[step, slot],
            send_rows.at[step, peer], recv_rows.at[step, slot], device_of(peer),
        )

    def total_near_copy():
        return send(total_out, total_near, send_total, recv_total_near, mate)

    def total_cross_copy():
        return send(total_out, total_in, send_total, recv_total_cross, across)

    some = cells // PARTS

    def cells_of(part):
        return pl.ds(pl.multiple_of(part * some, some), some)

    def every_part(act):
        def one(part, carry):
            act(part)
            return carry

        lax.fori_loop(0, PARTS, one, 0)

    def near_copy(step, part):
        span = cells_of(part)
        return send(
            sums_out.at[step, span], near_in.at[step, span],
            send_near.at[step, part], recv_near.at[step, part], mate,
        )

    def cross_copy(step, part):
        span = cells_of(part)
        return send(
            sums_out.at[step, span], cross_in.at[step, span],
            send_cross.at[step, part], recv_cross.at[step, part], across,
        )

    def back_copy(step, part):
        span = cells_of(part)
        return send(
            templates.at[step, span], templates.at[step, span],
            send_back.at[step, part], recv_back.at[step, part], mate,
        )

    def coadd_copy(step):
        start = pl.multiple_of((layer * CORES + 1 - core) * CELLS, CELLS)
        return send(
            templates.at[step, pl.ds(start, CELLS)], coadd_in.at[step],
            send_coadd.at[step], recv_coadd.at[step], (visit, layer * CORES + 1 - core),
        )

    def diffs_copy(step, peer, slot):
        return send(
            diffs.at[step, peer], diffs_in.at[step, slot],
            send_diffs.at[step, peer], recv_diffs.at[step, slot], device_of(peer),
        )

    for part in range(LOADS):
        for copy in load_copies(part):
            copy.start()

    peers(lambda peer: greet(device_of(peer)))
    greet(mate)
    pl.when(inner)(lambda: greet(across))

    segment = (owner_ref[...] * CELLS + cell_ref[...]).astype(jnp.float32)
    weight = inv_var_ref[...].astype(jnp.bfloat16).astype(jnp.float32)
    facts[...] = jnp.zeros_like(facts)
    facts[0:1, :] = jnp.concatenate([segment, segment], axis=1)
    facts[1:2, :] = jnp.concatenate([weight, weight], axis=1)

    unit = 4

    def match_unit(part, carry):
        first = part * unit
        usable = (mask[pl.ds(first, unit)] & 7) == 0
        masked = jnp.where(usable, pixels[pl.ds(first, unit)].astype(jnp.float32), 0.0)
        masked = masked.astype(jnp.bfloat16).reshape(unit * side_len, side_len)
        columns = jnp.dot(masked, right_ref[...], preferred_element_type=jnp.float32)
        columns = columns.astype(jnp.bfloat16)
        for n in range(unit):
            kernel_set = index_ref[first + n]
            left_parts = []
            for m in range(3):
                even, odd = bands_ref[2 * m], bands_ref[2 * m + 1]
                coef = [table_ref[3 * m + t, kernel_set] for t in range(3)]
                left_parts.append((coef[0] * even + coef[1] * odd).astype(jnp.bfloat16))
                left_parts.append((coef[2] * even).astype(jnp.bfloat16))
            left = jnp.concatenate(left_parts, axis=1)
            own = columns[n * side_len : (n + 1) * side_len]
            stacked = jnp.concatenate(
                [own[:, p * side_len : (p + 1) * side_len] for p in range(6)], axis=0
            )
            start = pl.multiple_of((first + n) * side_len, side_len)
            wide[pl.ds(start, side_len), :] = jnp.dot(left, stacked, preferred_element_type=jnp.float32)
        return carry

    for part in range(LOADS):
        for copy in load_copies(part):
            copy.wait()
        lax.fori_loop(part * load // unit, (part + 1) * load // unit, match_unit, 0)

    pl.semaphore_wait(barrier, jnp.where(inner, PLANE + 1, PLANE))
    peers(lambda peer: facts_copy(peer, me).start())

    def send_rows_of(step):
        def gather_rows(peer, carry):
            for k in range(PAIR):
                start = peer * ROWS + step * PAIR + k
                values = wide[pl.ds(start, blocks, stride=side_len), :].astype(jnp.bfloat16)
                rows[step, peer, :, k * side_len : (k + 1) * side_len] = values
            return carry

        lax.fori_loop(0, PLANE, gather_rows, 0)
        peers(lambda peer: rows_copy(step, peer, me).start())
        held[step, pl.ds(me, 1)] = rows[step, pl.ds(me, 1)]

    ahead = 2
    for step in range(ahead):
        send_rows_of(step)
    facts_in[pl.ds(me, 1)] = facts[...].reshape((1,) + facts.shape)
    peers(lambda peer: facts_copy(peer, peer).wait_recv())

    def make_pickers(pair, carry):
        first_lanes = lax.broadcasted_iota(jnp.int32, (1, lanes), 1) < blocks
        segment = jnp.where(first_lanes, facts_in[2 * pair, 0:1, :], facts_in[2 * pair + 1, 0:1, :])
        weight = jnp.where(first_lanes, facts_in[2 * pair, 1:2, :], facts_in[2 * pair + 1, 1:2, :])
        start = pl.multiple_of(pair * lanes, lanes)
        cell = lax.broadcasted_iota(jnp.int32, (cells, lanes), 0).astype(jnp.float32)
        weights[:, pl.ds(start, lanes)] = jnp.where(cell == segment, weight, 0.0).astype(jnp.bfloat16)
        weight_rows[:, pl.ds(start, lanes)] = jnp.broadcast_to(weight, (16, lanes)).astype(jnp.bfloat16)
        segment_column = jnp.broadcast_to(segment, (lanes, lanes)).T
        for c in range(cells // lanes):
            cell = lax.broadcasted_iota(jnp.int32, (lanes, lanes), 1) + c * lanes
            chosen = jnp.where(cell.astype(jnp.float32) == segment_column, 1.0, 0.0)
            picks[pl.ds(start, lanes), c * lanes : (c + 1) * lanes] = chosen.astype(jnp.bfloat16)
        return carry

    lax.fori_loop(0, PLANE // 2, make_pickers, 0)
    part_total = jnp.dot(weight_rows[...], picks[...], preferred_element_type=jnp.float32)
    total_out[...] = part_total[0:8]
    pl.when(outer)(lambda: total_near_copy().start())

    def add_up(step):
        peers(lambda peer: rows_copy(step, peer, peer).wait_recv())
        flat = held[step].reshape(total, width)
        part_sum = jnp.dot(weights[...], flat, preferred_element_type=jnp.float32)

        @pl.when(inner)
        def _():
            sums[step] = part_sum

        @pl.when(outer)
        def _():
            sums_out[step] = part_sum.astype(jnp.bfloat16)
            every_part(lambda part: near_copy(step, part).start())

    def join_totals():
        total_near_copy().wait_recv()
        total_out[...] += total_near[...]
        total_cross_copy().start()

    def join(step, part):
        near_copy(step, part).wait_recv()
        span = cells_of(part)
        joint = sums[step, span] + near_in[step, span].astype(jnp.float32)
        sums[step, span] = joint
        sums_out[step, span] = joint.astype(jnp.bfloat16)
        cross_copy(step, part).start()

    def get_scale():
        total_cross_copy().wait_recv()
        scale_row = 1.0 / jnp.maximum(total_out[0:1] + total_in[0:1], 1.0)
        for c in range(cells // lanes):
            scale[c * lanes : (c + 1) * lanes] = jnp.broadcast_to(
                scale_row[:, c * lanes : (c + 1) * lanes], (lanes, lanes)
            ).T

    def settle(step, part):
        cross_copy(step, part).wait_recv()
        span = cells_of(part)
        whole_sum = sums[step, span] + cross_in[step, span].astype(jnp.float32)
        for k in range(PAIR):
            lane = slice(k * side_len, (k + 1) * side_len)
            templates[step, span, lane] = (whole_sum[:, lane] * scale[span]).astype(jnp.bfloat16)
        back_copy(step, part).start()

    def take_off(step):
        flat = held[step].reshape(total, width)
        chosen = jnp.dot(picks[...], templates[step], preferred_element_type=jnp.float32)
        change = (flat.astype(jnp.float32) - chosen).astype(jnp.bfloat16)
        diffs[step] = change.reshape(PLANE, blocks, width)
        peers(lambda peer: diffs_copy(step, peer, me).start())
        coadd_copy(step).start()
        diffs_in[step, pl.ds(me, 1)] = diffs[step, pl.ds(me, 1)]

    rows_here = CORES * ROWS

    def finish(step):
        start = pl.multiple_of(patch * CELLS, CELLS)
        own = templates[step, pl.ds(start, CELLS)].astype(jnp.float32)
        for k in range(PAIR):
            row = core * ROWS + step * PAIR + k
            coadd_ref[pl.ds(row, CELLS, stride=rows_here), :] = own[:, k * side_len : (k + 1) * side_len]
        peers(lambda peer: diffs_copy(step, peer, peer).wait_recv())

        def spread(source, carry):
            values = diffs_in[step, source].astype(jnp.float32)
            for k in range(PAIR):
                row = source * ROWS + step * PAIR + k
                wide[pl.ds(row, blocks, stride=side_len), :] = values[
                    :, k * side_len : (k + 1) * side_len
                ]
            return carry

        lax.fori_loop(0, PLANE, spread, 0)
        coadd_copy(step).wait_recv()
        other = coadd_in[step].astype(jnp.float32)
        for k in range(PAIR):
            row = (1 - core) * ROWS + step * PAIR + k
            coadd_ref[pl.ds(row, CELLS, stride=rows_here), :] = other[:, k * side_len : (k + 1) * side_len]

    def one_step(step, carry):
        @pl.when(inner)
        def _():
            pl.when(step == 1)(join_totals)
            pl.when((step >= 1) & (step <= STEPS))(lambda: every_part(lambda part: join(step - 1, part)))
            pl.when(step == 2)(get_scale)
            pl.when((step >= 2) & (step <= STEPS + 1))(lambda: every_part(lambda part: settle(step - 2, part)))

        pl.when(step < STEPS)(lambda: add_up(step))
        pl.when(step + ahead < STEPS)(lambda: send_rows_of(step + ahead))

        late = jnp.where(inner, 2, 7)

        @pl.when((step >= late) & (step < STEPS + late))
        def _():
            pl.when(outer)(lambda: every_part(lambda part: back_copy(step - late, part).wait_recv()))
            take_off(step - late)

        last = late + 1
        pl.when((step >= last) & (step < STEPS + last))(lambda: finish(step - last))
        return carry

    lax.fori_loop(0, jnp.where(inner, STEPS + 3, STEPS + 8), one_step, 0)

    def narrow(part, carry):
        start = pl.multiple_of(part * 512, 512)
        difference_ref[pl.ds(start, 512), :] = wide[pl.ds(start, 512), :].astype(jnp.bfloat16)
        return carry

    lax.fori_loop(0, wide.shape[0] // 512, narrow, 0)

    peers(lambda peer: facts_copy(peer, me).wait_send())
    pl.when(inner)(lambda: total_cross_copy().wait_send())
    pl.when(outer)(lambda: total_near_copy().wait_send())

    def sent(step, carry):
        peers(lambda peer: rows_copy(step, peer, me).wait_send())
        peers(lambda peer: diffs_copy(step, peer, me).wait_send())
        coadd_copy(step).wait_send()

        @pl.when(inner)
        def _():
            every_part(lambda part: cross_copy(step, part).wait_send())
            every_part(lambda part: back_copy(step, part).wait_send())

        pl.when(outer)(lambda: every_part(lambda part: near_copy(step, part).wait_send()))
        return carry

    lax.fori_loop(0, STEPS, sent, 0)


def row_shards(pixels, mask_bits, inv_var, owner, cell, coef_index, coef_table):
    blocks, side_len = pixels.shape[0], pixels.shape[1]
    cells = lax.axis_size("patch") * CELLS
    total = PLANE * blocks
    width = PAIR * side_len
    bands = fixed_bands(side_len)
    right_bands = np.transpose(bands, (2, 0, 1)).reshape(side_len, 6 * side_len)
    bf16, f32 = jnp.bfloat16, jnp.float32
    dma = pltpu.SemaphoreType.DMA
    smem, vmem = pl.BlockSpec(memory_space=pltpu.SMEM), pl.BlockSpec(memory_space=pltpu.VMEM)
    coadd, difference = pl.pallas_call(
        trade_kernel,
        in_specs=[smem] * 2 + [vmem] * 5 + [pl.BlockSpec(memory_space=pl.ANY)] * 2,
        out_specs=[vmem] * 2,
        out_shape=[
            jax.ShapeDtypeStruct((CELLS * CORES * ROWS, side_len), f32),
            jax.ShapeDtypeStruct((blocks * side_len, side_len), bf16),
        ],
        scratch_shapes=[
            pltpu.VMEM((blocks, side_len, side_len), bf16),
            pltpu.VMEM((blocks, side_len, side_len), jnp.int32),
            pltpu.VMEM((STEPS, PLANE, blocks, width), bf16),
            pltpu.VMEM((STEPS, PLANE, blocks, width), bf16),
            pltpu.VMEM((STEPS, cells, width), f32),
            pltpu.VMEM((STEPS, cells, width), bf16),
            pltpu.VMEM((STEPS, cells, width), bf16),
            pltpu.VMEM((STEPS, cells, width), bf16),
            pltpu.VMEM((STEPS, cells, width), bf16),
            pltpu.VMEM((STEPS, CELLS, width), bf16),
            pltpu.VMEM((STEPS, PLANE, blocks, width), bf16),
            pltpu.VMEM((STEPS, PLANE, blocks, width), bf16),
            pltpu.VMEM((cells, total), bf16),
            pltpu.VMEM((total, cells), bf16),
            pltpu.VMEM((blocks * side_len, side_len), f32),
            pltpu.VMEM((8, 2 * blocks), f32),
            pltpu.VMEM((PLANE, 8, 2 * blocks), f32),
            pltpu.VMEM((16, total), bf16),
            pltpu.VMEM((8, cells), f32),
            pltpu.VMEM((8, cells), f32),
            pltpu.VMEM((8, cells), f32),
            pltpu.VMEM((cells, side_len), f32),
            dma((LOADS,)),
            dma((LOADS,)),
            dma((STEPS, PLANE)),
            dma((STEPS, PLANE)),
            dma((PLANE,)),
            dma((PLANE,)),
            dma,
            dma,
            dma,
        ]
        + [dma((STEPS, PARTS))] * 6
        + [dma((STEPS,))] * 2
        + [dma((STEPS, PLANE))] * 2,
        compiler_params=pltpu.CompilerParams(
            collective_id=0, has_side_effects=True, vmem_limit_bytes=58 * 2**20
        ),
    )(
        coef_index, coef_table.T,
        inv_var.reshape(1, blocks), owner.reshape(1, blocks), cell.reshape(1, blocks),
        jnp.asarray(right_bands, dtype=bf16), jnp.asarray(bands), pixels, mask_bits,
    )
    return (
        coadd.reshape(CELLS, CORES * ROWS, side_len),
        difference.reshape(blocks, side_len, side_len),
    )


def solution(mesh):
    placed = (
        P(("visit", "patch"), None, None),
        P(("visit", "patch"), None, None),
        P(("visit", "patch")),
        P(("visit", "patch")),
        P(("visit", "patch")),
        P(("visit", "patch")),
        P(),
    )
    fits = mesh.shape["visit"] * CORES == PLANE and mesh.shape["patch"] == 4 * CORES
    return jax.shard_map(
        row_shards if fits else shards,
        mesh=mesh,
        in_specs=placed,
        out_specs=(P("patch", "visit", None), P(("visit", "patch"), None, None)),
        check_vma=False,
    )
```
